32 devices in a mesh: crop: 2 (over x), ia: 8 (over z, y), ja: 2 (over core).
Axes of the slice: x: 2, y: 2, z: 4, core: 2. Of those that a mesh axis runs over, the one named last changes fastest.
Arguments:
- pair_in: bfloat16 [512, 256, 128], P(('crop', 'ia', 'ja')), parts along dimension 0, may hold values from -6 to 6
- tri_sum: bfloat16 [512, 256, 128], P(('crop', 'ia', 'ja')), parts along dimension 0, may hold values from -6 to 6
- pair_mid: bfloat16 [512, 256, 128], P(('crop', 'ia', 'ja')), parts along dimension 0, may hold values from -6 to 6
- pair_grad: bfloat16 [512, 256, 128], P(('crop', 'ia', 'ja')), parts along dimension 0, may hold values from -6 to 6
- residue_mask: int32 [512], P('crop'), parts along dimension 0, may hold values from 0 to 1, as said below
- tri_gain: float32 [128], replicated, may hold values from 0.1 to 1.9
- w_left: bfloat16 [128, 256], replicated, may hold values from -0.5 to 0.5
- w_right: bfloat16 [128, 256], replicated, may hold values from -0.5 to 0.5
- w_tgate: bfloat16 [128, 128], replicated, may hold values from -0.5 to 0.5
- sum_gain: float32 [128], replicated, may hold values from 0.1 to 1.9
- w_tout: bfloat16 [128, 128], replicated, may hold values from -0.5 to 0.5
- att_gain: float32 [128], replicated, may hold values from 0.1 to 1.9
- w_qkvg: bfloat16 [128, 512], replicated, may hold values from -0.5 to 0.5
- w_bias: bfloat16 [128, 4], replicated, may hold values from -0.5 to 0.5
- w_aout: bfloat16 [128, 128], replicated, may hold values from -0.5 to 0.5
Outputs:
- pair_in_grad: float32 [512, 256, 128], P(('crop', 'ia', 'ja')), parts along dimension 0
The draws below stay inside these ranges and needn't reach their ends.
There are 2 independent parts, one for each index of `crop`. The reference program is written for one: setup_inputs(seed, part) draws one part's arguments, and reference() takes and returns one part's arrays. A program takes and returns all parts, laid end to end along the dimension named above; an argument that names none is the same for every part. Nothing has to cross between parts.
Inputs may be any that keep to these rules, and one draw needn't show every extreme that they name: `residue_mask`: 1 for the first residues of the crop, half of the 256 residues or more, and 0 for the padding that follows them.
All inputs are finite; a program needn't handle non-finite values.
Results may differ from the reference program's by a relative error of at most 0.009.
Values may be sent and summed in bfloat16 or wider, within the bound.
A program may use at most 128 MiB of HBM per device.

```python
import jax
import jax.numpy as jnp
from jax import lax

C = 128
H = 4
DH = 32
N = 256


def draw_residue_mask(key, part):
    key = jax.random.fold_in(key, 11)
    valid_count = jax.random.randint(key, (), N // 2, N + 1)
    return (jnp.arange(N) < valid_count).astype(jnp.int32)


def raised(result, key, source, target, blocks, factor):
    def block_of(position):
        return (jnp.arange(result.shape[position]) // (result.shape[position] // blocks)).reshape((-1,) + (1,) * (result.ndim - 1 - position))

    near = jax.random.permutation(key, blocks)[block_of(target)]
    other_side = (block_of(target) + blocks // 2) % blocks
    return jnp.where((block_of(source) == near) | (block_of(source) == other_side), factor * result, result)


def level_of(key, extent, shards, smallest, largest):
    gain = 1.0
    for position, parts in shards:
        draws = jax.random.uniform(jax.random.fold_in(jax.random.fold_in(key, 6), position), (parts,), jnp.float32, smallest / len(shards), largest / len(shards))
        gain = gain * jnp.repeat(jnp.exp(draws), extent[position] // parts).reshape((-1,) + (1,) * (len(extent) - 1 - position))
    return gain


def noise(key, dims, deviation, bound, pieces=(), dtype=jnp.bfloat16):
    entries = jax.random.normal(key, dims, jnp.float32) * deviation
    if len(pieces) > 0:
        entries = level_of(key, dims, pieces, -0.22, 0.18) * entries
    return jnp.clip(entries, min=-bound, max=bound).astype(dtype)


def gaussian_with(own_key, shape, width, bound, shards, heavy, kind=jnp.bfloat16):
    array = width * jax.random.normal(own_key, shape, jnp.float32)
    if shards:
        array = array * level_of(own_key, shape, shards, -0.22, 0.18)
    return jnp.clip(raised(array, jax.random.fold_in(own_key, 3), *heavy), -bound, bound).astype(kind)


def setup_inputs(seed: int = 0, part: int = 0) -> dict:
    key_of = jax.random.split(jax.random.key(seed), 16)
    own_keys = jax.random.split(jax.random.fold_in(key_of[15], part), 16)
    return {
        "pair_in": noise(own_keys[0], (N, N, C), 1.0, 6.0, ((0, 16),)),
        "tri_sum": noise(own_keys[1], (N, N, C), 1.0, 6.0, ((0, 16),)),
        "pair_mid": noise(own_keys[2], (N, N, C), 1.0, 6.0, ((0, 16),)),
        "pair_grad": gaussian_with(own_keys[3], (N, N, C), 1.0, 6.0, ((0, 16),), (0, 1, 16, 2.0)),
        "residue_mask": draw_residue_mask(jax.random.fold_in(jax.random.fold_in(key_of[15], part), 71), part),
        "tri_gain": jnp.clip(1.0 + 0.18 * jax.random.normal(key_of[5], (C,), jnp.float32), 0.1, 1.9),
        "w_left": noise(key_of[6], (C, 2 * C), C ** -0.5, 0.5),
        "w_right": noise(key_of[7], (C, 2 * C), C ** -0.5, 0.5),
        "w_tgate": noise(key_of[8], (C, C), C ** -0.5, 0.5),
        "sum_gain": jnp.clip(1.0 + 0.18 * jax.random.normal(key_of[9], (C,), jnp.float32), 0.1, 1.9),
        "w_tout": noise(key_of[10], (C, C), C ** -0.5, 0.5),
        "att_gain": jnp.clip(1.0 + 0.18 * jax.random.normal(key_of[11], (C,), jnp.float32), 0.1, 1.9),
        "w_qkvg": noise(key_of[12], (C, 4 * C), C ** -0.5, 0.5),
        "w_bias": noise(key_of[13], (C, H), C ** -0.5, 0.5),
        "w_aout": noise(key_of[14], (C, C), C ** -0.5, 0.5),
    }


EPSILON = 1e-05

def normalize(values_in, gain_row):
    average = lax.optimization_barrier(jnp.mean(values_in, axis=-1, keepdims=True))
    centred = values_in - average
    second = lax.optimization_barrier(jnp.mean(centred * centred, axis=-1, keepdims=True))
    return centred * lax.rsqrt(second + EPSILON) * gain_row

def normalize_grad(values_in, gain_row, cotangent):
    pullback = jax.vjp(lambda inside: normalize(inside, gain_row), values_in)[1]
    return pullback(cotangent)[0]

def rounded(values_in):
    return lax.optimization_barrier(values_in.astype(jnp.bfloat16)).astype(jnp.float32)

def reference(pair_in, tri_sum, pair_mid, pair_grad, residue_mask, tri_gain, w_left, w_right, w_tgate, sum_gain, w_tout, att_gain, w_qkvg, w_bias, w_aout):
    key_mask = residue_mask.astype(jnp.float32)
    score_scale = DH ** (-0.5)
    mid_full = pair_mid.astype(jnp.float32)
    normed_mid = normalize(mid_full, att_gain).astype(jnp.bfloat16)
    bias_cells = jnp.dot(normed_mid.reshape(N * N, C), w_bias, preferred_element_type=jnp.float32)
    bias_full = rounded(bias_cells).reshape(N, N, H).transpose(2, 0, 1)

    def attend_row(running, row_in):
        normed_row, grad_row = row_in
        projected = jnp.dot(normed_row, w_qkvg, preferred_element_type=jnp.float32)
        queries = rounded(projected[:, :C]).reshape(N, H, DH)
        key_rows = rounded(projected[:, C:2 * C]).reshape(N, H, DH)
        value_rows = rounded(projected[:, 2 * C:3 * C]).reshape(N, H, DH)
        att_gate = jax.nn.sigmoid(projected[:, 3 * C:])
        scores = jnp.einsum('jhd,khd->hjk', queries, key_rows) * score_scale + bias_full
        exp_scores = jnp.exp(scores) * key_mask
        probs = exp_scores / lax.optimization_barrier(jnp.sum(exp_scores, axis=-1, keepdims=True))
        probs_b = rounded(probs)
        attended = jnp.einsum('hjk,khd->jhd', probs_b, value_rows).reshape(N, C)
        gated_grad = jnp.dot(grad_row, w_aout.T, preferred_element_type=jnp.float32)
        logit_grad = gated_grad * attended * att_gate * (1.0 - att_gate)
        out_grad = rounded(gated_grad * att_gate).reshape(N, H, DH)
        prob_grad = jnp.einsum('jhd,khd->hjk', out_grad, value_rows)
        score_grad = probs * (prob_grad - lax.optimization_barrier(jnp.sum(probs * prob_grad, axis=-1, keepdims=True)))
        score_b = rounded(score_grad)
        query_grad = jnp.einsum('hjk,khd->jhd', score_b, key_rows) * score_scale
        key_grad = jnp.einsum('hjk,jhd->khd', score_b, queries) * score_scale
        value_grad = jnp.einsum('hjk,jhd->khd', probs_b, out_grad)
        proj_grad = jnp.concatenate([query_grad.reshape(N, C), key_grad.reshape(N, C), value_grad.reshape(N, C), logit_grad], axis=-1).astype(jnp.bfloat16)
        normed_grad = jnp.dot(proj_grad, w_qkvg.T, preferred_element_type=jnp.float32)
        return (running + score_grad, normed_grad)
    bias_grad, normed_grad = lax.scan(attend_row, jnp.zeros((H, N, N), jnp.float32), (normed_mid, pair_grad))
    normed_grad = normed_grad + jnp.einsum('hjk,ch->jkc', bias_grad, w_bias.astype(jnp.float32), precision=lax.Precision.HIGHEST)
    mid_grad = pair_grad.astype(jnp.float32) + normalize_grad(mid_full, att_gain, normed_grad)
    in_full = pair_in.astype(jnp.float32)
    normed_in = normalize(in_full, tri_gain).astype(jnp.bfloat16).reshape(N * N, C)
    cell_mask = (key_mask[:, None] * key_mask[None, :])[:, :, None]
    left_proj = jnp.dot(normed_in, w_left, preferred_element_type=jnp.float32).reshape(N, N, 2 * C)
    left_gate = jax.nn.sigmoid(left_proj[..., :C])
    left_act = rounded(cell_mask * left_gate * left_proj[..., C:])
    right_proj = jnp.dot(normed_in, w_right, preferred_element_type=jnp.float32).reshape(N, N, 2 * C)
    right_gate = jax.nn.sigmoid(right_proj[..., :C])
    right_act = rounded(cell_mask * right_gate * right_proj[..., C:])
    tri_gate = jax.nn.sigmoid(jnp.dot(normed_in, w_tgate, preferred_element_type=jnp.float32)).reshape(N, N, C)
    sum_full = tri_sum.astype(jnp.float32)
    sum_normed = normalize(sum_full, sum_gain).astype(jnp.bfloat16).reshape(N * N, C)
    tri_out = jnp.dot(sum_normed, w_tout, preferred_element_type=jnp.float32).reshape(N, N, C)
    tout_grad = (mid_grad * tri_gate).astype(jnp.bfloat16).reshape(N * N, C)
    gate_back = (mid_grad * tri_out * tri_gate * (1.0 - tri_gate)).astype(jnp.bfloat16).reshape(N * N, C)
    summed_grad = jnp.dot(tout_grad, w_tout.T, preferred_element_type=jnp.float32).reshape(N, N, C)
    sum_grad = rounded(normalize_grad(sum_full, sum_gain, summed_grad))
    left_grad = rounded(jnp.einsum('ijc,jkc->ikc', sum_grad, right_act))
    right_grad = rounded(jnp.einsum('ijc,ikc->jkc', sum_grad, left_act))
    left_back = jnp.concatenate([left_grad * cell_mask * left_proj[..., C:] * left_gate * (1.0 - left_gate), left_grad * cell_mask * left_gate], axis=-1).astype(jnp.bfloat16).reshape(N * N, 2 * C)
    right_back = jnp.concatenate([right_grad * cell_mask * right_proj[..., C:] * right_gate * (1.0 - right_gate), right_grad * cell_mask * right_gate], axis=-1).astype(jnp.bfloat16).reshape(N * N, 2 * C)
    normed_in_grad = jnp.dot(left_back, w_left.T, preferred_element_type=jnp.float32)
    normed_in_grad = normed_in_grad + jnp.dot(right_back, w_right.T, preferred_element_type=jnp.float32)
    normed_in_grad = normed_in_grad + jnp.dot(gate_back, w_tgate.T, preferred_element_type=jnp.float32)
    return mid_grad + normalize_grad(in_full, tri_gain, normed_in_grad.reshape(N, N, C))
```

```python
import functools
import math

import jax
import jax.numpy as jnp
from jax import lax
from jax.experimental import pallas as pl
from jax.experimental.pallas import tpu as pltpu
from jax.sharding import PartitionSpec as P

EPSILON = 1e-05
F32 = jnp.float32
BF16 = jnp.bfloat16
VMEM_BYTES = 48 * 1024 * 1024
AXES = ("ia", "ja")


def dot(a, b):
    return jnp.dot(a, b, preferred_element_type=F32)


def dot_t(a, b):
    return lax.dot_general(a, b, (((1,), (1,)), ((), ())), preferred_element_type=F32)


def standardize(v):
    average = jnp.mean(v, axis=-1, keepdims=True)
    centred = v - average
    second = jnp.mean(centred * centred, axis=-1, keepdims=True)
    rstd = lax.rsqrt(second + EPSILON)
    return centred * rstd, rstd


def norm_grad(unit, rstd, gain, cotangent):
    g = cotangent * gain
    return rstd * (
        g
        - jnp.mean(g, axis=-1, keepdims=True)
        - unit * jnp.mean(g * unit, axis=-1, keepdims=True)
    )


def rows_of(ref):
    block = ref[...]
    return block.reshape(block.shape[0] * block.shape[1], block.shape[2])


def put_planes(ref, r, value, split):
    if split:
        ref[:, r] = value.reshape(ref.shape[0], ref.shape[2], ref.shape[3]).astype(BF16)
    else:
        ref[r] = value.astype(BF16)


def get_planes(ref, r, split):
    if split:
        value = ref[:, r].astype(F32)
        return value.reshape(value.shape[0] * value.shape[1], value.shape[2])
    return ref[r].astype(F32)


def edge_kernel(split, pin_ref, cell_ref, gain_ref, wt_ref, left_ref, right_ref):
    block, length, channels = pin_ref.shape
    unit, _ = standardize(rows_of(pin_ref).astype(F32))
    normed = (unit * gain_ref[...]).astype(BF16)
    proj = dot_t(wt_ref[...], normed)
    for r in range(block):
        part = proj[:, r * length : (r + 1) * length]
        cell = cell_ref[r]
        left = cell * jax.nn.sigmoid(part[:channels]) * part[channels : 2 * channels]
        right = (
            cell * jax.nn.sigmoid(part[2 * channels : 3 * channels]) * part[3 * channels :]
        )
        put_planes(left_ref, r, left, split)
        put_planes(right_ref, r, right, split)


def attention_kernel(
    heads,
    mid_ref,
    grad_ref,
    gain_ref,
    wt_ref,
    wkv_ref,
    wqg_ref,
    wtkv_ref,
    waout_ref,
    bias_ref,
    out_ref,
    bias_out_ref,
    q_block,
    o_block,
    acc,
):
    step = pl.program_id(0)
    length, channels = mid_ref.shape[1:]
    dim = channels // heads
    scale = dim ** (-0.5)

    @pl.when(step == 0)
    def _():
        q_block[...] = jnp.zeros_like(q_block)
        o_block[...] = jnp.zeros_like(o_block)
        acc[...] = jnp.zeros_like(acc)

    unit, _ = standardize(mid_ref[0].astype(F32))
    normed = (unit * gain_ref[...]).astype(BF16)
    proj = dot_t(wt_ref[...], normed)
    kv = dot(normed, wkv_ref[...]).astype(BF16)
    keys, values = kv[:, :channels], kv[:, channels:]
    keys_t = proj[channels : 2 * channels].astype(BF16)
    values_t = proj[2 * channels : 3 * channels].astype(BF16)
    queries_t = proj[:channels].astype(BF16)
    gate = jax.nn.sigmoid(proj[3 * channels :])
    gated = dot_t(waout_ref[...], grad_ref[0])
    out_t = (gated * gate).astype(BF16)
    for h in range(heads):
        rows = slice(h * dim, (h + 1) * dim)
        q_block[h, rows] = queries_t[rows]
        o_block[h, rows] = out_t[rows]
    attended, query_grads = [], []
    key_grad = jnp.zeros((length, channels), F32)
    value_grad = jnp.zeros((length, channels), F32)
    for h in range(heads):
        rows = slice(h * dim, (h + 1) * dim)
        scores = dot(keys, q_block[h])
        e = jnp.exp2(scores * (scale * math.log2(math.e)) + bias_ref[h])
        probs = e * (1.0 / jnp.sum(e, axis=0, keepdims=True))
        probs_b = probs.astype(BF16)
        prob_grad = dot(values, o_block[h])
        weighted = probs * prob_grad
        score_grad = weighted - probs * jnp.sum(weighted, axis=0, keepdims=True)
        score_b = score_grad.astype(BF16)
        acc[h] += score_grad
        attended.append(dot(values_t[rows], probs_b))
        query_grads.append(dot(keys_t[rows], score_b))
        key_grad += dot_t(score_b, q_block[h])
        value_grad += dot_t(probs_b, o_block[h])
    attended = jnp.concatenate(attended, axis=0)
    query_grad = jnp.concatenate(query_grads, axis=0) * scale
    logit_grad = gated * attended * gate * (1.0 - gate)
    qg = jnp.concatenate([query_grad, logit_grad], axis=0).astype(BF16)
    kv_grad = jnp.concatenate([key_grad * scale, value_grad], axis=1).astype(BF16)
    out_ref[0] = dot(kv_grad, wtkv_ref[...]) + dot(wqg_ref[...], qg).T

    @pl.when(step == pl.num_programs(0) - 1)
    def _():
        for h in range(heads):
            bias_out_ref[h] = acc[h].T.astype(BF16)


def middle_kernel(
    split,
    heads,
    ng_ref,
    band_ref,
    wb_ref,
    mid_ref,
    grad_ref,
    pin_ref,
    sum_ref,
    att_gain_ref,
    tri_gain_ref,
    sum_gain_ref,
    wtgate_ref,
    wtout_ref,
    wtout_t_ref,
    mid_out_ref,
    back_ref,
    planes_ref,
):
    block, length, channels = mid_ref.shape
    bias = []
    for r in range(block):
        band = band_ref[r].T
        part = band[:, 0:1] * wb_ref[0:1]
        for h in range(1, heads):
            part = part + band[:, h : h + 1] * wb_ref[h : h + 1]
        bias.append(part)
    bias = jnp.concatenate(bias, axis=0)
    unit, rstd = standardize(rows_of(mid_ref).astype(F32))
    mid_grad = rows_of(grad_ref).astype(F32) + norm_grad(
        unit, rstd, att_gain_ref[...], rows_of(ng_ref) + bias
    )
    unit, _ = standardize(rows_of(pin_ref).astype(F32))
    gate = jax.nn.sigmoid(dot((unit * tri_gain_ref[...]).astype(BF16), wtgate_ref[...]))
    unit, rstd = standardize(rows_of(sum_ref).astype(F32))
    tri_out = dot((unit * sum_gain_ref[...]).astype(BF16), wtout_ref[...])
    gated = mid_grad * gate
    summed = dot(gated.astype(BF16), wtout_t_ref[...])
    back = gated * tri_out * (1.0 - gate)
    mid_out_ref[...] = mid_grad.reshape(block, length, channels)
    back_ref[...] = back.astype(BF16).reshape(block, length, channels)
    sum_grad = norm_grad(unit, rstd, sum_gain_ref[...], summed)
    for r in range(block):
        put_planes(planes_ref, r, sum_grad[r * length : (r + 1) * length].T, split)


def left_kernel(grad_ref, right_ref, out_ref):
    planes = grad_ref.shape[0]
    outs = []
    for c in range(planes):
        outs.append(dot(grad_ref[c], right_ref[c]))
    if planes % 8 == 0:
        out_ref[...] = jnp.swapaxes(jnp.stack(outs, axis=0), 0, 1).astype(BF16)
    else:
        for c in range(planes):
            out_ref[c] = outs[c].astype(BF16)


def right_kernel(grad_ref, left_ref, out_ref):
    planes = grad_ref.shape[0]
    outs = []
    for c in range(planes):
        outs.append(dot(grad_ref[c].T, left_ref[c]))
    if planes % 8 == 0:
        out_ref[...] = jnp.swapaxes(jnp.stack(outs, axis=0), 0, 1).astype(BF16)
    else:
        for c in range(planes):
            out_ref[c] = outs[c].astype(BF16)


def final_kernel(
    split,
    left_ref,
    right_ref,
    back_ref,
    mid_ref,
    pin_ref,
    cell_ref,
    gain_ref,
    wt_ref,
    wleft_ref,
    wright_ref,
    wtgate_t_ref,
    out_ref,
):
    block, length, channels = pin_ref.shape
    unit, rstd = standardize(rows_of(pin_ref).astype(F32))
    normed = (unit * gain_ref[...]).astype(BF16)
    proj = dot_t(wt_ref[...], normed)

    def backward(grad, part):
        s = jax.nn.sigmoid(part[:channels])
        gs = grad * s
        return jnp.concatenate([gs * part[channels:] * (1.0 - s), gs], axis=0).astype(BF16)

    grads = []
    for r in range(block):
        part = proj[:, r * length : (r + 1) * length]
        cell = cell_ref[r]
        left = backward(get_planes(left_ref, r, split) * cell, part[: 2 * channels])
        right = backward(get_planes(right_ref, r, split) * cell, part[2 * channels :])
        grads.append((dot(wleft_ref[...], left) + dot(wright_ref[...], right)).T)
    total = jnp.concatenate(grads, axis=0) + dot(rows_of(back_ref), wtgate_t_ref[...])
    result = rows_of(mid_ref) + norm_grad(unit, rstd, gain_ref[...], total)
    out_ref[...] = result.reshape(block, length, channels)


def whole(array):
    zeros = (0,) * array.ndim
    return pl.BlockSpec(array.shape, lambda i: zeros)


def banded(array, block):
    rest = array.shape[1:]
    zeros = (0,) * len(rest)
    return pl.BlockSpec((block,) + rest, lambda i: (i,) + zeros)


def params():
    return pltpu.CompilerParams(
        dimension_semantics=("arbitrary",), vmem_limit_bytes=VMEM_BYTES
    )


def per_device(
    pair_in,
    tri_sum,
    pair_mid,
    pair_grad,
    residue_mask,
    tri_gain,
    w_left,
    w_right,
    w_tgate,
    sum_gain,
    w_tout,
    att_gain,
    w_qkvg,
    w_bias,
    w_aout,
):
    rows, length, channels = pair_in.shape
    heads = w_bias.shape[1]
    devices = length // rows
    group = channels // devices
    split = group % 8 == 0
    block = math.gcd(rows, 4)
    key_mask = residue_mask.astype(F32)
    band_index = lax.axis_index(AXES)
    row_mask = lax.dynamic_slice_in_dim(key_mask, band_index * rows, rows)
    cell = (row_mask[:, None] * key_mask[None, :])[:, None, :]
    tri_gain, sum_gain, att_gain = tri_gain[None], sum_gain[None], att_gain[None]
    wt_edges = jnp.concatenate([w_left.T, w_right.T], axis=0)
    wt_qkvg = w_qkvg.T
    w_kv = w_qkvg[:, channels : 3 * channels]
    w_qg = jnp.concatenate([w_qkvg[:, :channels], w_qkvg[:, 3 * channels :]], axis=1)
    wt_kv = wt_qkvg[channels : 3 * channels]

    unit, _ = standardize(pair_mid.astype(F32))
    normed_mid = (unit * att_gain).astype(BF16)
    bias_local = lax.dot_general(
        w_bias, normed_mid, (((0,), (2,)), ((), ())), preferred_element_type=F32
    ).astype(BF16)
    bias_full = lax.all_gather(bias_local, AXES, axis=1, tiled=True)
    bias_t = jnp.swapaxes(bias_full, 1, 2).astype(F32) * math.log2(math.e)
    bias_t = bias_t + jnp.where(residue_mask > 0, 0.0, -1e30)[None, :, None]

    if split:
        plane_shape = jax.ShapeDtypeStruct((devices, rows, group, length), BF16)
        plane_spec = pl.BlockSpec((devices, block, group, length), lambda i: (0, i, 0, 0))
    else:
        plane_shape = jax.ShapeDtypeStruct((rows, channels, length), BF16)
        plane_spec = pl.BlockSpec((block, channels, length), lambda i: (i, 0, 0))

    def spread(planes):
        if not split:
            planes = jnp.swapaxes(planes.reshape(rows, devices, group, length), 0, 1)
        gathered = lax.all_to_all(planes, AXES, split_axis=0, concat_axis=0, tiled=True)
        return jnp.swapaxes(gathered.reshape(length, group, length), 0, 1)

    def collect(planes):
        if not split:
            planes = jnp.swapaxes(planes, 0, 1)
        planes = planes.reshape(devices, rows, group, length)
        back = lax.all_to_all(planes, AXES, split_axis=0, concat_axis=0, tiled=True)
        if not split:
            back = jnp.swapaxes(back, 0, 1).reshape(rows, channels, length)
        return back

    def run(kernel, args, banded_count, out_shape, out_specs, special=()):
        specs = [banded(a, block) for a in args[:banded_count]]
        specs += [whole(a) for a in args[banded_count:]]
        for position, spec in special:
            specs[position] = spec
        return pl.pallas_call(
            kernel,
            grid=(rows // block,),
            in_specs=specs,
            out_specs=out_specs,
            out_shape=out_shape,
            compiler_params=params(),
        )(*args)

    left_act, right_act = run(
        functools.partial(edge_kernel, split),
        (pair_in, cell, tri_gain, wt_edges),
        2,
        (plane_shape, plane_shape),
        (plane_spec, plane_spec),
    )
    left_planes, right_planes = spread(left_act), spread(right_act)

    attention_args = (
        pair_mid,
        pair_grad,
        att_gain,
        wt_qkvg,
        w_kv,
        w_qg,
        wt_kv,
        w_aout,
        bias_t,
    )
    normed_grad, bias_part = pl.pallas_call(
        functools.partial(attention_kernel, heads),
        grid=(rows,),
        in_specs=[banded(a, 1) for a in attention_args[:2]]
        + [whole(a) for a in attention_args[2:]],
        out_specs=(
            pl.BlockSpec((1, length, channels), lambda i: (i, 0, 0)),
            pl.BlockSpec((heads, length, length), lambda i: (0, 0, 0)),
        ),
        out_shape=(
            jax.ShapeDtypeStruct((rows, length, channels), F32),
            jax.ShapeDtypeStruct((heads, length, length), BF16),
        ),
        scratch_shapes=[
            pltpu.VMEM((heads, channels, length), BF16),
            pltpu.VMEM((heads, channels, length), BF16),
            pltpu.VMEM((heads, length, length), F32),
        ],
        compiler_params=params(),
        cost_estimate=pl.CostEstimate(
            flops=rows * heads * 12 * length * length * channels,
            bytes_accessed=rows * length * channels * 8,
            transcendentals=rows * heads * length * length,
        ),
    )(*attention_args)
    bias_part = jnp.swapaxes(bias_part.reshape(heads, devices, rows, length), 0, 1)
    bias_parts = lax.all_to_all(bias_part, AXES, split_axis=0, concat_axis=0, tiled=True)
    band = jnp.swapaxes(jnp.sum(bias_parts.astype(F32), axis=0), 0, 1)
    band = jnp.pad(band, ((0, 0), (0, -heads % 8), (0, 0)))

    row_spec = pl.BlockSpec((block, length, channels), lambda i: (i, 0, 0))
    row_shape = jax.ShapeDtypeStruct((rows, length, channels), F32)
    wb_t = jnp.pad(w_bias.astype(F32).T, ((0, -heads % 8), (0, 0)))
    mid_grad, gate_back, sum_grad = pl.pallas_call(
        functools.partial(middle_kernel, split, heads),
        grid=(rows // block,),
        in_specs=[banded(normed_grad, block), banded(band, block), whole(wb_t)]
        + [row_spec] * 4
        + [whole(a) for a in (att_gain, tri_gain, sum_gain, w_tgate, w_tout, w_tout)],
        out_specs=(row_spec, row_spec, plane_spec),
        out_shape=(row_shape, jax.ShapeDtypeStruct(row_shape.shape, BF16), plane_shape),
        compiler_params=params(),
    )(
        normed_grad,
        band,
        wb_t,
        pair_mid,
        pair_grad,
        pair_in,
        tri_sum,
        att_gain,
        tri_gain,
        sum_gain,
        w_tgate,
        w_tout,
        w_tout.T,
    )
    grad_planes = spread(sum_grad)

    def product(kernel, other):
        shape = (length, group, length) if split else (group, length, length)
        return pl.pallas_call(
            kernel,
            in_specs=[pl.BlockSpec(memory_space=pltpu.VMEM)] * 2,
            out_specs=pl.BlockSpec(memory_space=pltpu.VMEM),
            out_shape=jax.ShapeDtypeStruct(shape, BF16),
            compiler_params=pltpu.CompilerParams(vmem_limit_bytes=VMEM_BYTES),
        )(grad_planes, other)

    left_grad = collect(product(left_kernel, right_planes))
    right_grad = collect(product(right_kernel, left_planes))
    return run(
        functools.partial(final_kernel, split),
        (
            left_grad,
            right_grad,
            gate_back,
            mid_grad,
            pair_in,
            cell,
            tri_gain,
            wt_edges,
            w_left,
            w_right,
            w_tgate.T,
        ),
        6,
        row_shape,
        row_spec,
        special=((0, plane_spec), (1, plane_spec)),
    )


def solution(mesh):
    rows = P(("crop", "ia", "ja"), None, None)
    placed = (rows, rows, rows, rows, P("crop")) + (P(),) * 10
    return jax.shard_map(
        per_device, mesh=mesh, in_specs=placed, out_specs=rows, check_vma=False
    )
```

```python
import functools
import math

import jax
import jax.numpy as jnp
from jax import lax
from jax.experimental import pallas as pl
from jax.experimental.pallas import tpu as pltpu
from jax.sharding import PartitionSpec as P

EPSILON = 1e-05
F32 = jnp.float32
BF16 = jnp.bfloat16
VMEM_BYTES = 48 * 1024 * 1024
AXES = ("ia", "ja")


def dot(a, b):
    return jnp.dot(a, b, preferred_element_type=F32)


def dot_t(a, b):
    return lax.dot_general(a, b, (((1,), (1,)), ((), ())), preferred_element_type=F32)


def standardize(v):
    average = jnp.mean(v, axis=-1, keepdims=True)
    centred = v - average
    second = jnp.mean(centred * centred, axis=-1, keepdims=True)
    rstd = lax.rsqrt(second + EPSILON)
    return centred * rstd, rstd


def norm_grad(unit, rstd, gain, cotangent):
    g = cotangent * gain
    return rstd * (
        g
        - jnp.mean(g, axis=-1, keepdims=True)
        - unit * jnp.mean(g * unit, axis=-1, keepdims=True)
    )


def rows_of(ref):
    block = ref[...]
    return block.reshape(block.shape[0] * block.shape[1], block.shape[2])


def put_planes(ref, r, value, split):
    if split:
        ref[:, r] = value.reshape(ref.shape[0], ref.shape[2], ref.shape[3]).astype(BF16)
    else:
        ref[r] = value.astype(BF16)


def get_planes(ref, r, split):
    if split:
        value = ref[:, r].astype(F32)
        return value.reshape(value.shape[0] * value.shape[1], value.shape[2])
    return ref[r].astype(F32)


def edge_kernel(split, pin_ref, cell_ref, gain_ref, wt_ref, left_ref, right_ref):
    block, length, channels = pin_ref.shape
    unit, _ = standardize(rows_of(pin_ref).astype(F32))
    normed = (unit * gain_ref[...]).astype(BF16)
    proj = dot_t(wt_ref[...], normed)
    for r in range(block):
        part = proj[:, r * length : (r + 1) * length]
        cell = cell_ref[r]
        left = cell * jax.nn.sigmoid(part[:channels]) * part[channels : 2 * channels]
        right = (
            cell * jax.nn.sigmoid(part[2 * channels : 3 * channels]) * part[3 * channels :]
        )
        put_planes(left_ref, r, left, split)
        put_planes(right_ref, r, right, split)


def attention_row(
    heads, normed, grad_row, wt_ref, wkv_ref, wqg_ref, wtkv_ref, waout_ref, bias_ref, q_block, o_block, acc
):
    length, channels = normed.shape
    dim = channels // heads
    scale = dim ** (-0.5)
    proj = dot_t(wt_ref[...], normed)
    kv = dot(normed, wkv_ref[...]).astype(BF16)
    keys, values = kv[:, :channels], kv[:, channels:]
    keys_t = proj[channels : 2 * channels].astype(BF16)
    values_t = proj[2 * channels : 3 * channels].astype(BF16)
    queries_t = proj[:channels].astype(BF16)
    gate = jax.nn.sigmoid(proj[3 * channels :])
    gated = dot_t(waout_ref[...], grad_row)
    out_t = (gated * gate).astype(BF16)
    for h in range(heads):
        rows = slice(h * dim, (h + 1) * dim)
        q_block[h, rows] = queries_t[rows]
        o_block[h, rows] = out_t[rows]
    attended, query_grads = [], []
    key_grad = jnp.zeros((length, channels), F32)
    value_grad = jnp.zeros((length, channels), F32)
    for h in range(heads):
        rows = slice(h * dim, (h + 1) * dim)
        scores = dot(keys, q_block[h])
        e = jnp.exp2(scores * (scale * math.log2(math.e)) + bias_ref[h])
        probs = e * (1.0 / jnp.sum(e, axis=0, keepdims=True))
        probs_b = probs.astype(BF16)
        prob_grad = dot(values, o_block[h])
        weighted = probs * prob_grad
        score_grad = weighted - probs * jnp.sum(weighted, axis=0, keepdims=True)
        score_b = score_grad.astype(BF16)
        acc[h] += score_grad
        attended.append(dot(values_t[rows], probs_b))
        query_grads.append(dot(keys_t[rows], score_b))
        key_grad += dot_t(score_b, q_block[h])
        value_grad += dot_t(probs_b, o_block[h])
    attended = jnp.concatenate(attended, axis=0)
    query_grad = jnp.concatenate(query_grads, axis=0) * scale
    logit_grad = gated * attended * gate * (1.0 - gate)
    qg = jnp.concatenate([query_grad, logit_grad], axis=0).astype(BF16)
    kv_grad = jnp.concatenate([key_grad * scale, value_grad], axis=1).astype(BF16)
    return dot(kv_grad, wtkv_ref[...]) + dot(wqg_ref[...], qg).T


def attention_kernel(
    heads,
    mid_ref,
    grad_ref,
    gain_ref,
    wt_ref,
    wkv_ref,
    wqg_ref,
    wtkv_ref,
    waout_ref,
    bias_ref,
    out_ref,
    bias_out_ref,
    q_block,
    o_block,
    acc,
):
    step = pl.program_id(0)

    @pl.when(step == 0)
    def _():
        q_block[...] = jnp.zeros_like(q_block)
        o_block[...] = jnp.zeros_like(o_block)
        acc[...] = jnp.zeros_like(acc)

    unit, _ = standardize(mid_ref[0].astype(F32))
    normed = (unit * gain_ref[...]).astype(BF16)
    out_ref[0] = attention_row(
        heads, normed, grad_ref[0], wt_ref, wkv_ref, wqg_ref, wtkv_ref, waout_ref, bias_ref, q_block, o_block, acc
    )

    @pl.when(step == pl.num_programs(0) - 1)
    def _():
        for h in range(heads):
            bias_out_ref[h] = acc[h].T.astype(BF16)


def enter(me, count, second):
    barrier = pltpu.get_barrier_semaphore()

    def greet(p, carry):
        other = lax.rem(me + p, count)
        pl.semaphore_signal(
            barrier, inc=1, device_id=place(other, second), device_id_type=pl.DeviceIdType.MESH
        )
        return carry

    lax.fori_loop(1, count, greet, 0)
    pl.semaphore_wait(barrier, count - 1)


def place(index, second):
    return {"ia": lax.div(index, second), "ja": lax.rem(index, second)}


class Exchange:
    def __init__(self, source, target, send, recv, slot, me, count, second, same=False):
        self.source, self.target, self.same = source, target, same
        self.send, self.recv, self.slot = send, recv, slot
        self.me, self.count, self.second = me, count, second

    def copy(self, p):
        other = lax.rem(self.me + p, self.count)
        return pltpu.make_async_remote_copy(
            src_ref=self.source if self.same else self.source.at[other],
            dst_ref=self.target.at[self.me],
            send_sem=self.send.at[self.slot, p],
            recv_sem=self.recv.at[self.slot, p],
            device_id=place(other, self.second),
            device_id_type=pl.DeviceIdType.MESH,
        )

    def start(self):
        def go(p, carry):
            self.copy(p).start()
            return carry

        lax.fori_loop(1, self.count, go, 0)
        if self.same:
            self.target[self.me] = self.source[...]
        else:
            self.target[self.me] = self.source[self.me]

    def wait(self):
        def go(p, carry):
            self.copy(p).wait()
            return carry

        lax.fori_loop(1, self.count, go, 0)


def position():
    second = lax.axis_size("ja")
    return (
        lax.axis_index("ia") * second + lax.axis_index("ja"),
        lax.axis_size("ia") * second,
        second,
    )


def first_kernel(
    heads,
    in_ref,
    mid_ref,
    grad_ref,
    cell_ref,
    mask_ref,
    tri_gain_ref,
    att_gain_ref,
    wt_edges_ref,
    wb_ref,
    wt_ref,
    wkv_ref,
    wqg_ref,
    wtkv_ref,
    waout_ref,
    out_ref,
    band_ref,
    left_out_ref,
    right_out_ref,
    normed_ref,
    bias_send,
    bias_recv,
    left_send,
    left_recv,
    right_send,
    right_recv,
    part_send,
    part_recv,
    bias_ref,
    q_block,
    o_block,
    acc,
    send,
    recv,
):
    rows, length, channels = in_ref.shape
    block = math.gcd(rows, 4)
    me, count, second = position()
    link = (send, recv)
    bias_x = Exchange(bias_send, bias_recv, *link, 0, me, count, second, same=True)
    left_x = Exchange(left_send, left_recv, *link, 1, me, count, second)
    right_x = Exchange(right_send, right_recv, *link, 2, me, count, second)
    part_x = Exchange(part_send, part_recv, *link, 3, me, count, second)

    bias_rows = []
    for b in range(rows // block):
        part = slice(b * block, (b + 1) * block)
        unit, _ = standardize(mid_ref[part].reshape(block * length, channels).astype(F32))
        normed = (unit * att_gain_ref[...]).astype(BF16)
        normed_ref[part] = normed.reshape(block, length, channels)
        bias = dot_t(wb_ref[...], normed)
        bias_rows += [bias[:, r * length : (r + 1) * length] for r in range(block)]
    for h in range(heads):
        bias_send[h] = jnp.concatenate([b[h : h + 1] for b in bias_rows], axis=0).astype(BF16)
    enter(me, count, second)
    bias_x.start()

    def edges(b, carry):
        part = pl.ds(b * block, block)
        unit, _ = standardize(in_ref[part].reshape(block * length, channels).astype(F32))
        proj = dot_t(wt_edges_ref[...], (unit * tri_gain_ref[...]).astype(BF16))
        for r in range(block):
            p = proj[:, r * length : (r + 1) * length]
            cell = cell_ref[b * block + r]
            left = cell * jax.nn.sigmoid(p[:channels]) * p[channels : 2 * channels]
            right = cell * jax.nn.sigmoid(p[2 * channels : 3 * channels]) * p[3 * channels :]
            shape = (count, channels // count, length)
            left_send[:, b * block + r] = left.reshape(shape).astype(BF16)
            right_send[:, b * block + r] = right.reshape(shape).astype(BF16)
        return carry

    lax.fori_loop(0, rows // block, edges, 0)
    bias_x.wait()
    left_x.start()
    right_x.start()
    q_block[...] = jnp.zeros_like(q_block)
    o_block[...] = jnp.zeros_like(o_block)
    acc[...] = jnp.zeros_like(acc)
    for h in range(heads):
        full = bias_recv[:, h].astype(F32).reshape(length, length)
        bias_ref[h] = (full * math.log2(math.e) + mask_ref[...]).T

    def attend(i, carry):
        out_ref[i] = attention_row(
            heads,
            normed_ref[i],
            grad_ref[i],
            wt_ref,
            wkv_ref,
            wqg_ref,
            wtkv_ref,
            waout_ref,
            bias_ref,
            q_block,
            o_block,
            acc,
        )
        return carry

    lax.fori_loop(0, rows, attend, 0)
    for h in range(heads):
        part_send[:, h] = acc[h].T.reshape(count, rows, length).astype(BF16)
    part_x.start()
    left_x.wait()
    to_planes(left_recv, left_out_ref)
    right_x.wait()
    to_planes(right_recv, right_out_ref)
    part_x.wait()
    for h in range(heads):
        band_ref[h] = jnp.sum(part_recv[:, h].astype(F32), axis=0)


def to_planes(received, planes_ref):
    count, rows = received.shape[:2]

    def move(s, carry):
        value = jnp.swapaxes(received[s].astype(F32), 0, 1).astype(BF16)
        planes_ref[:, pl.ds(pl.multiple_of(s * rows, rows), rows), :] = value
        return carry

    lax.fori_loop(0, count, move, 0)


def middle_kernel(
    split,
    heads,
    ng_ref,
    band_ref,
    wb_ref,
    mid_ref,
    grad_ref,
    pin_ref,
    sum_ref,
    att_gain_ref,
    tri_gain_ref,
    sum_gain_ref,
    wtgate_ref,
    wtout_ref,
    wtout_t_ref,
    mid_out_ref,
    back_ref,
    planes_ref,
):
    block, length, channels = mid_ref.shape
    bias = []
    for r in range(block):
        band = band_ref[r].T
        part = band[:, 0:1] * wb_ref[0:1]
        for h in range(1, heads):
            part = part + band[:, h : h + 1] * wb_ref[h : h + 1]
        bias.append(part)
    bias = jnp.concatenate(bias, axis=0)
    unit, rstd = standardize(rows_of(mid_ref).astype(F32))
    mid_grad = rows_of(grad_ref).astype(F32) + norm_grad(
        unit, rstd, att_gain_ref[...], rows_of(ng_ref) + bias
    )
    unit, _ = standardize(rows_of(pin_ref).astype(F32))
    gate = jax.nn.sigmoid(dot((unit * tri_gain_ref[...]).astype(BF16), wtgate_ref[...]))
    unit, rstd = standardize(rows_of(sum_ref).astype(F32))
    tri_out = dot((unit * sum_gain_ref[...]).astype(BF16), wtout_ref[...])
    gated = mid_grad * gate
    summed = dot(gated.astype(BF16), wtout_t_ref[...])
    back = gated * tri_out * (1.0 - gate)
    mid_out_ref[...] = mid_grad.reshape(block, length, channels)
    back_ref[...] = back.astype(BF16).reshape(block, length, channels)
    sum_grad = norm_grad(unit, rstd, sum_gain_ref[...], summed)
    for r in range(block):
        put_planes(planes_ref, r, sum_grad[r * length : (r + 1) * length].T, split)


def left_kernel(grad_ref, right_ref, out_ref):
    planes = grad_ref.shape[0]
    outs = []
    for c in range(planes):
        outs.append(dot(grad_ref[c], right_ref[c]))
    if planes % 8 == 0:
        out_ref[...] = jnp.swapaxes(jnp.stack(outs, axis=0), 0, 1).astype(BF16)
    else:
        for c in range(planes):
            out_ref[c] = outs[c].astype(BF16)


def right_kernel(grad_ref, left_ref, out_ref):
    planes = grad_ref.shape[0]
    outs = []
    for c in range(planes):
        outs.append(dot(grad_ref[c].T, left_ref[c]))
    if planes % 8 == 0:
        out_ref[...] = jnp.swapaxes(jnp.stack(outs, axis=0), 0, 1).astype(BF16)
    else:
        for c in range(planes):
            out_ref[c] = outs[c].astype(BF16)


def final_kernel(
    split,
    left_ref,
    right_ref,
    back_ref,
    mid_ref,
    pin_ref,
    cell_ref,
    gain_ref,
    wt_ref,
    wleft_ref,
    wright_ref,
    wtgate_t_ref,
    out_ref,
):
    block, length, channels = pin_ref.shape
    unit, rstd = standardize(rows_of(pin_ref).astype(F32))
    normed = (unit * gain_ref[...]).astype(BF16)
    proj = dot_t(wt_ref[...], normed)

    def backward(grad, part):
        s = jax.nn.sigmoid(part[:channels])
        gs = grad * s
        return jnp.concatenate([gs * part[channels:] * (1.0 - s), gs], axis=0).astype(BF16)

    grads = []
    for r in range(block):
        part = proj[:, r * length : (r + 1) * length]
        cell = cell_ref[r]
        left = backward(get_planes(left_ref, r, split) * cell, part[: 2 * channels])
        right = backward(get_planes(right_ref, r, split) * cell, part[2 * channels :])
        grads.append((dot(wleft_ref[...], left) + dot(wright_ref[...], right)).T)
    total = jnp.concatenate(grads, axis=0) + dot(rows_of(back_ref), wtgate_t_ref[...])
    result = rows_of(mid_ref) + norm_grad(unit, rstd, gain_ref[...], total)
    out_ref[...] = result.reshape(block, length, channels)


def whole(array):
    zeros = (0,) * array.ndim
    return pl.BlockSpec(array.shape, lambda i: zeros)


def banded(array, block):
    rest = array.shape[1:]
    zeros = (0,) * len(rest)
    return pl.BlockSpec((block,) + rest, lambda i: (i,) + zeros)


def params():
    return pltpu.CompilerParams(
        dimension_semantics=("arbitrary",), vmem_limit_bytes=VMEM_BYTES
    )


def per_device(
    pair_in,
    tri_sum,
    pair_mid,
    pair_grad,
    residue_mask,
    tri_gain,
    w_left,
    w_right,
    w_tgate,
    sum_gain,
    w_tout,
    att_gain,
    w_qkvg,
    w_bias,
    w_aout,
):
    rows, length, channels = pair_in.shape
    heads = w_bias.shape[1]
    devices = length // rows
    group = channels // devices
    split = group % 8 == 0
    block = math.gcd(rows, 4)
    key_mask = residue_mask.astype(F32)
    band_index = lax.axis_index(AXES)
    row_mask = lax.dynamic_slice_in_dim(key_mask, band_index * rows, rows)
    cell = (row_mask[:, None] * key_mask[None, :])[:, None, :]
    tri_gain, sum_gain, att_gain = tri_gain[None], sum_gain[None], att_gain[None]
    wt_edges = jnp.concatenate([w_left.T, w_right.T], axis=0)
    wt_qkvg = w_qkvg.T
    w_kv = w_qkvg[:, channels : 3 * channels]
    w_qg = jnp.concatenate([w_qkvg[:, :channels], w_qkvg[:, 3 * channels :]], axis=1)
    wt_kv = wt_qkvg[channels : 3 * channels]

    if split:
        plane_shape = jax.ShapeDtypeStruct((devices, rows, group, length), BF16)
        plane_spec = pl.BlockSpec((devices, block, group, length), lambda i: (0, i, 0, 0))
    else:
        plane_shape = jax.ShapeDtypeStruct((rows, channels, length), BF16)
        plane_spec = pl.BlockSpec((block, channels, length), lambda i: (i, 0, 0))

    def spread(planes):
        if not split:
            planes = jnp.swapaxes(planes.reshape(rows, devices, group, length), 0, 1)
        gathered = lax.all_to_all(planes, AXES, split_axis=0, concat_axis=0, tiled=True)
        return jnp.swapaxes(gathered.reshape(length, group, length), 0, 1)

    def collect(planes):
        if not split:
            planes = jnp.swapaxes(planes, 0, 1)
        planes = planes.reshape(devices, rows, group, length)
        back = lax.all_to_all(planes, AXES, split_axis=0, concat_axis=0, tiled=True)
        if not split:
            back = jnp.swapaxes(back, 0, 1).reshape(rows, channels, length)
        return back

    def run(kernel, args, banded_count, out_shape, out_specs, special=()):
        specs = [banded(a, block) for a in args[:banded_count]]
        specs += [whole(a) for a in args[banded_count:]]
        for position, spec in special:
            specs[position] = spec
        return pl.pallas_call(
            kernel,
            grid=(rows // block,),
            in_specs=specs,
            out_specs=out_specs,
            out_shape=out_shape,
            compiler_params=params(),
        )(*args)

    if split:
        operands = (
            pair_in,
            pair_mid,
            pair_grad,
            cell,
            jnp.where(residue_mask > 0, 0.0, -1e30)[None],
            tri_gain,
            att_gain,
            wt_edges,
            jnp.pad(w_bias.T, ((0, -heads % 16), (0, 0))),
            wt_qkvg,
            w_kv,
            w_qg,
            wt_kv,
            w_aout,
        )
        vmem = pl.BlockSpec(memory_space=pltpu.VMEM)
        planes = jax.ShapeDtypeStruct((group, length, length), BF16)
        ones = pltpu.VMEM((devices, rows, group, length), BF16)
        parts = pltpu.VMEM((devices, heads, rows, length), BF16)
        normed_grad, band, left_planes, right_planes = pl.pallas_call(
            functools.partial(first_kernel, heads),
            in_specs=[vmem] * len(operands),
            out_specs=[vmem] * 4,
            out_shape=(
                jax.ShapeDtypeStruct((rows, length, channels), F32),
                jax.ShapeDtypeStruct((heads, rows, length), F32),
                planes,
                planes,
            ),
            scratch_shapes=[
                pltpu.VMEM((rows, length, channels), BF16),
                pltpu.VMEM((heads, rows, length), BF16),
                parts,
                ones,
                ones,
                ones,
                ones,
                parts,
                parts,
                pltpu.VMEM((heads, length, length), F32),
                pltpu.VMEM((heads, channels, length), BF16),
                pltpu.VMEM((heads, channels, length), BF16),
                pltpu.VMEM((heads, length, length), F32),
                pltpu.SemaphoreType.DMA((4, devices)),
                pltpu.SemaphoreType.DMA((4, devices)),
            ],
            compiler_params=pltpu.CompilerParams(
                collective_id=0, has_side_effects=True, vmem_limit_bytes=VMEM_BYTES
            ),
        )(*operands)
        band = jnp.swapaxes(band, 0, 1)
    else:
        unit, _ = standardize(pair_mid.astype(F32))
        normed_mid = (unit * att_gain).astype(BF16)
        bias_local = lax.dot_general(
            w_bias, normed_mid, (((0,), (2,)), ((), ())), preferred_element_type=F32
        ).astype(BF16)
        bias_full = lax.all_gather(bias_local, AXES, axis=1, tiled=True)
        bias_t = jnp.swapaxes(bias_full, 1, 2).astype(F32) * math.log2(math.e)
        bias_t = bias_t + jnp.where(residue_mask > 0, 0.0, -1e30)[None, :, None]

        left_act, right_act = run(
            functools.partial(edge_kernel, split),
            (pair_in, cell, tri_gain, wt_edges),
            2,
            (plane_shape, plane_shape),
            (plane_spec, plane_spec),
        )
        left_planes, right_planes = spread(left_act), spread(right_act)

        attention_args = (
            pair_mid,
            pair_grad,
            att_gain,
            wt_qkvg,
            w_kv,
            w_qg,
            wt_kv,
            w_aout,
            bias_t,
        )
        normed_grad, bias_part = pl.pallas_call(
            functools.partial(attention_kernel, heads),
            grid=(rows,),
            in_specs=[banded(a, 1) for a in attention_args[:2]]
            + [whole(a) for a in attention_args[2:]],
            out_specs=(
                pl.BlockSpec((1, length, channels), lambda i: (i, 0, 0)),
                pl.BlockSpec((heads, length, length), lambda i: (0, 0, 0)),
            ),
            out_shape=(
                jax.ShapeDtypeStruct((rows, length, channels), F32),
                jax.ShapeDtypeStruct((heads, length, length), BF16),
            ),
            scratch_shapes=[
                pltpu.VMEM((heads, channels, length), BF16),
                pltpu.VMEM((heads, channels, length), BF16),
                pltpu.VMEM((heads, length, length), F32),
            ],
            compiler_params=params(),
            cost_estimate=pl.CostEstimate(
                flops=rows * heads * 12 * length * length * channels,
                bytes_accessed=rows * length * channels * 8,
                transcendentals=rows * heads * length * length,
            ),
        )(*attention_args)
        bias_part = jnp.swapaxes(bias_part.reshape(heads, devices, rows, length), 0, 1)
        bias_parts = lax.all_to_all(bias_part, AXES, split_axis=0, concat_axis=0, tiled=True)
        band = jnp.swapaxes(jnp.sum(bias_parts.astype(F32), axis=0), 0, 1)
    band = jnp.pad(band, ((0, 0), (0, -heads % 8), (0, 0)))

    row_spec = pl.BlockSpec((block, length, channels), lambda i: (i, 0, 0))
    row_shape = jax.ShapeDtypeStruct((rows, length, channels), F32)
    wb_t = jnp.pad(w_bias.astype(F32).T, ((0, -heads % 8), (0, 0)))
    mid_grad, gate_back, sum_grad = pl.pallas_call(
        functools.partial(middle_kernel, split, heads),
        grid=(rows // block,),
        in_specs=[banded(normed_grad, block), banded(band, block), whole(wb_t)]
        + [row_spec] * 4
        + [whole(a) for a in (att_gain, tri_gain, sum_gain, w_tgate, w_tout, w_tout)],
        out_specs=(row_spec, row_spec, plane_spec),
        out_shape=(row_shape, jax.ShapeDtypeStruct(row_shape.shape, BF16), plane_shape),
        compiler_params=params(),
    )(
        normed_grad,
        band,
        wb_t,
        pair_mid,
        pair_grad,
        pair_in,
        tri_sum,
        att_gain,
        tri_gain,
        sum_gain,
        w_tgate,
        w_tout,
        w_tout.T,
    )
    grad_planes = spread(sum_grad)

    def product(kernel, other):
        shape = (length, group, length) if split else (group, length, length)
        return pl.pallas_call(
            kernel,
            in_specs=[pl.BlockSpec(memory_space=pltpu.VMEM)] * 2,
            out_specs=pl.BlockSpec(memory_space=pltpu.VMEM),
            out_shape=jax.ShapeDtypeStruct(shape, BF16),
            compiler_params=pltpu.CompilerParams(vmem_limit_bytes=VMEM_BYTES),
        )(grad_planes, other)

    left_grad = collect(product(left_kernel, right_planes))
    right_grad = collect(product(right_kernel, left_planes))
    return run(
        functools.partial(final_kernel, split),
        (
            left_grad,
            right_grad,
            gate_back,
            mid_grad,
            pair_in,
            cell,
            tri_gain,
            wt_edges,
            w_left,
            w_right,
            w_tgate.T,
        ),
        6,
        row_shape,
        row_spec,
        special=((0, plane_spec), (1, plane_spec)),
    )


def solution(mesh):
    rows = P(("crop", "ia", "ja"), None, None)
    placed = (rows, rows, rows, rows, P("crop")) + (P(),) * 10
    return jax.shard_map(
        per_device, mesh=mesh, in_specs=placed, out_specs=rows, check_vma=False
    )
```

```python
import functools
import math

import jax
import jax.numpy as jnp
from jax import lax
from jax.experimental import pallas as pl
from jax.experimental.pallas import tpu as pltpu
from jax.sharding import PartitionSpec as P

EPSILON = 1e-05
F32 = jnp.float32
BF16 = jnp.bfloat16
VMEM_BYTES = 48 * 1024 * 1024
AXES = ("ia", "ja")


def dot(a, b):
    return jnp.dot(a, b, preferred_element_type=F32)


def dot_t(a, b):
    return lax.dot_general(a, b, (((1,), (1,)), ((), ())), preferred_element_type=F32)


def standardize(v):
    average = jnp.mean(v, axis=-1, keepdims=True)
    centred = v - average
    second = jnp.mean(centred * centred, axis=-1, keepdims=True)
    rstd = lax.rsqrt(second + EPSILON)
    return centred * rstd, rstd


def norm_grad(unit, rstd, gain, cotangent):
    g = cotangent * gain
    return rstd * (
        g
        - jnp.mean(g, axis=-1, keepdims=True)
        - unit * jnp.mean(g * unit, axis=-1, keepdims=True)
    )


def rows_of(ref):
    block = ref[...]
    return block.reshape(block.shape[0] * block.shape[1], block.shape[2])


def put_planes(ref, r, value, split):
    if split:
        ref[:, r] = value.reshape(ref.shape[0], ref.shape[2], ref.shape[3]).astype(BF16)
    else:
        ref[r] = value.astype(BF16)


def get_planes(ref, r, split):
    if split:
        value = ref[:, r].astype(F32)
        return value.reshape(value.shape[0] * value.shape[1], value.shape[2])
    return ref[r].astype(F32)


def edge_kernel(split, pin_ref, cell_ref, gain_ref, wt_ref, left_ref, right_ref):
    block, length, channels = pin_ref.shape
    unit, _ = standardize(rows_of(pin_ref).astype(F32))
    normed = (unit * gain_ref[...]).astype(BF16)
    proj = dot_t(wt_ref[...], normed)
    for r in range(block):
        part = proj[:, r * length : (r + 1) * length]
        cell = cell_ref[r]
        left = cell * jax.nn.sigmoid(part[:channels]) * part[channels : 2 * channels]
        right = (
            cell * jax.nn.sigmoid(part[2 * channels : 3 * channels]) * part[3 * channels :]
        )
        put_planes(left_ref, r, left, split)
        put_planes(right_ref, r, right, split)


def attention_row(
    heads, normed, grad_row, wt_ref, wkv_ref, wqg_ref, wtkv_ref, waout_ref, bias_ref, q_block, o_block, acc
):
    length, channels = normed.shape
    dim = channels // heads
    scale = dim ** (-0.5)
    proj = dot_t(wt_ref[...], normed)
    kv = dot(normed, wkv_ref[...]).astype(BF16)
    keys, values = kv[:, :channels], kv[:, channels:]
    keys_t = proj[channels : 2 * channels].astype(BF16)
    values_t = proj[2 * channels : 3 * channels].astype(BF16)
    queries_t = proj[:channels].astype(BF16)
    gate = jax.nn.sigmoid(proj[3 * channels :])
    gated = dot_t(waout_ref[...], grad_row)
    out_t = (gated * gate).astype(BF16)
    for h in range(heads):
        rows = slice(h * dim, (h + 1) * dim)
        q_block[h, rows] = queries_t[rows]
        o_block[h, rows] = out_t[rows]
    attended, query_grads = [], []
    key_grad = jnp.zeros((length, channels), F32)
    value_grad = jnp.zeros((length, channels), F32)
    for h in range(heads):
        rows = slice(h * dim, (h + 1) * dim)
        scores = dot(keys, q_block[h])
        e = jnp.exp2(scores * (scale * math.log2(math.e)) + bias_ref[h])
        probs = e * (1.0 / jnp.sum(e, axis=0, keepdims=True))
        probs_b = probs.astype(BF16)
        prob_grad = dot(values, o_block[h])
        weighted = probs * prob_grad
        score_grad = weighted - probs * jnp.sum(weighted, axis=0, keepdims=True)
        score_b = score_grad.astype(BF16)
        acc[h] += score_grad
        attended.append(dot(values_t[rows], probs_b))
        query_grads.append(dot(keys_t[rows], score_b))
        key_grad += dot_t(score_b, q_block[h])
        value_grad += dot_t(probs_b, o_block[h])
    attended = jnp.concatenate(attended, axis=0)
    query_grad = jnp.concatenate(query_grads, axis=0) * scale
    logit_grad = gated * attended * gate * (1.0 - gate)
    qg = jnp.concatenate([query_grad, logit_grad], axis=0).astype(BF16)
    kv_grad = jnp.concatenate([key_grad * scale, value_grad], axis=1).astype(BF16)
    return dot(kv_grad, wtkv_ref[...]) + dot(wqg_ref[...], qg).T


def attention_kernel(
    heads,
    mid_ref,
    grad_ref,
    gain_ref,
    wt_ref,
    wkv_ref,
    wqg_ref,
    wtkv_ref,
    waout_ref,
    bias_ref,
    out_ref,
    bias_out_ref,
    q_block,
    o_block,
    acc,
):
    step = pl.program_id(0)

    @pl.when(step == 0)
    def _():
        q_block[...] = jnp.zeros_like(q_block)
        o_block[...] = jnp.zeros_like(o_block)
        acc[...] = jnp.zeros_like(acc)

    unit, _ = standardize(mid_ref[0].astype(F32))
    normed = (unit * gain_ref[...]).astype(BF16)
    out_ref[0] = attention_row(
        heads, normed, grad_ref[0], wt_ref, wkv_ref, wqg_ref, wtkv_ref, waout_ref, bias_ref, q_block, o_block, acc
    )

    @pl.when(step == pl.num_programs(0) - 1)
    def _():
        for h in range(heads):
            bias_out_ref[h] = acc[h].T.astype(BF16)


def enter(me, count, second):
    barrier = pltpu.get_barrier_semaphore()

    def greet(p, carry):
        other = lax.rem(me + p, count)
        pl.semaphore_signal(
            barrier, inc=1, device_id=place(other, second), device_id_type=pl.DeviceIdType.MESH
        )
        return carry

    lax.fori_loop(1, count, greet, 0)
    pl.semaphore_wait(barrier, count - 1)


def place(index, second):
    return {"ia": lax.div(index, second), "ja": lax.rem(index, second)}


class Exchange:
    def __init__(self, source, target, send, recv, slot, me, count, second, same=False, part=None):
        self.source, self.target, self.same, self.part = source, target, same, part
        self.send, self.recv, self.slot = send, recv, slot
        self.me, self.count, self.second = me, count, second

    def copy(self, p):
        other = lax.rem(self.me + p, self.count)
        source = self.source if self.same else self.source.at[other]
        target = self.target.at[self.me]
        if self.part is not None:
            source, target = source.at[self.part], target.at[self.part]
        return pltpu.make_async_remote_copy(
            src_ref=source,
            dst_ref=target,
            send_sem=self.send.at[self.slot, p],
            recv_sem=self.recv.at[self.slot, p],
            device_id=place(other, self.second),
            device_id_type=pl.DeviceIdType.MESH,
        )

    def start(self):
        def go(p, carry):
            self.copy(p).start()
            return carry

        lax.fori_loop(1, self.count, go, 0)
        if self.same:
            self.target[self.me] = self.source[...]
        elif self.part is not None:
            self.target[self.me, self.part] = self.source[self.me, self.part]
        else:
            self.target[self.me] = self.source[self.me]

    def wait(self):
        def go(p, carry):
            self.copy(p).wait()
            return carry

        lax.fori_loop(1, self.count, go, 0)


def position():
    second = lax.axis_size("ja")
    return (
        lax.axis_index("ia") * second + lax.axis_index("ja"),
        lax.axis_size("ia") * second,
        second,
    )


def first_kernel(
    heads,
    in_ref,
    mid_ref,
    grad_ref,
    cell_ref,
    mask_ref,
    tri_gain_ref,
    att_gain_ref,
    wt_edges_ref,
    wb_ref,
    wt_ref,
    wkv_ref,
    wqg_ref,
    wtkv_ref,
    waout_ref,
    out_ref,
    band_ref,
    left_out_ref,
    right_out_ref,
    normed_ref,
    bias_send,
    bias_recv,
    left_send,
    left_recv,
    right_send,
    right_recv,
    part_send,
    part_recv,
    bias_ref,
    q_block,
    o_block,
    acc,
    send,
    recv,
):
    rows, length, channels = in_ref.shape
    block = math.gcd(rows, 4)
    me, count, second = position()
    link = (send, recv)
    bias_x = Exchange(bias_send, bias_recv, *link, 0, me, count, second, same=True)
    left_x = Exchange(left_send, left_recv, *link, 1, me, count, second)
    right_x = Exchange(right_send, right_recv, *link, 2, me, count, second)
    part_x = Exchange(part_send, part_recv, *link, 3, me, count, second)

    bias_rows = []
    for b in range(rows // block):
        part = slice(b * block, (b + 1) * block)
        unit, _ = standardize(mid_ref[part].reshape(block * length, channels).astype(F32))
        normed = (unit * att_gain_ref[...]).astype(BF16)
        normed_ref[part] = normed.reshape(block, length, channels)
        bias = dot_t(wb_ref[...], normed)
        bias_rows += [bias[:, r * length : (r + 1) * length] for r in range(block)]
    for h in range(heads):
        bias_send[h] = jnp.concatenate([b[h : h + 1] for b in bias_rows], axis=0).astype(BF16)
    enter(me, count, second)
    bias_x.start()

    def edges(b, carry):
        part = pl.ds(b * block, block)
        unit, _ = standardize(in_ref[part].reshape(block * length, channels).astype(F32))
        proj = dot_t(wt_edges_ref[...], (unit * tri_gain_ref[...]).astype(BF16))
        for r in range(block):
            p = proj[:, r * length : (r + 1) * length]
            cell = cell_ref[b * block + r]
            left = cell * jax.nn.sigmoid(p[:channels]) * p[channels : 2 * channels]
            right = cell * jax.nn.sigmoid(p[2 * channels : 3 * channels]) * p[3 * channels :]
            shape = (count, channels // count, length)
            left_send[:, b * block + r] = left.reshape(shape).astype(BF16)
            right_send[:, b * block + r] = right.reshape(shape).astype(BF16)
        return carry

    lax.fori_loop(0, rows // block, edges, 0)
    bias_x.wait()
    left_x.start()
    right_x.start()
    q_block[...] = jnp.zeros_like(q_block)
    o_block[...] = jnp.zeros_like(o_block)
    acc[...] = jnp.zeros_like(acc)
    for h in range(heads):
        full = bias_recv[:, h].astype(F32).reshape(length, length)
        bias_ref[h] = (full * math.log2(math.e) + mask_ref[...]).T

    def attend(i, carry):
        out_ref[i] = attention_row(
            heads,
            normed_ref[i],
            grad_ref[i],
            wt_ref,
            wkv_ref,
            wqg_ref,
            wtkv_ref,
            waout_ref,
            bias_ref,
            q_block,
            o_block,
            acc,
        )
        return carry

    lax.fori_loop(0, rows, attend, 0)
    for h in range(heads):
        part_send[:, h] = acc[h].T.reshape(count, rows, length).astype(BF16)
    part_x.start()
    left_x.wait()
    to_planes(left_recv, left_out_ref)
    right_x.wait()
    to_planes(right_recv, right_out_ref)
    part_x.wait()
    for h in range(heads):
        band_ref[h] = jnp.sum(part_recv[:, h].astype(F32), axis=0)


def to_planes(received, planes_ref):
    count, rows = received.shape[:2]

    def move(s, carry):
        value = jnp.swapaxes(received[s].astype(F32), 0, 1).astype(BF16)
        planes_ref[:, pl.ds(pl.multiple_of(s * rows, rows), rows), :] = value
        return carry

    lax.fori_loop(0, count, move, 0)


def middle_kernel(
    split,
    heads,
    ng_ref,
    band_ref,
    wb_ref,
    mid_ref,
    grad_ref,
    pin_ref,
    sum_ref,
    att_gain_ref,
    tri_gain_ref,
    sum_gain_ref,
    wtgate_ref,
    wtout_ref,
    wtout_t_ref,
    mid_out_ref,
    back_ref,
    planes_ref,
):
    block, length, channels = mid_ref.shape
    bias = []
    for r in range(block):
        band = band_ref[r].T
        part = band[:, 0:1] * wb_ref[0:1]
        for h in range(1, heads):
            part = part + band[:, h : h + 1] * wb_ref[h : h + 1]
        bias.append(part)
    bias = jnp.concatenate(bias, axis=0)
    unit, rstd = standardize(rows_of(mid_ref).astype(F32))
    mid_grad = rows_of(grad_ref).astype(F32) + norm_grad(
        unit, rstd, att_gain_ref[...], rows_of(ng_ref) + bias
    )
    unit, _ = standardize(rows_of(pin_ref).astype(F32))
    gate = jax.nn.sigmoid(dot((unit * tri_gain_ref[...]).astype(BF16), wtgate_ref[...]))
    unit, rstd = standardize(rows_of(sum_ref).astype(F32))
    tri_out = dot((unit * sum_gain_ref[...]).astype(BF16), wtout_ref[...])
    gated = mid_grad * gate
    summed = dot(gated.astype(BF16), wtout_t_ref[...])
    back = gated * tri_out * (1.0 - gate)
    mid_out_ref[...] = mid_grad.reshape(block, length, channels)
    back_ref[...] = back.astype(BF16).reshape(block, length, channels)
    sum_grad = norm_grad(unit, rstd, sum_gain_ref[...], summed)
    for r in range(block):
        put_planes(planes_ref, r, sum_grad[r * length : (r + 1) * length].T, split)


def second_kernel(
    heads,
    ng_ref,
    band_ref,
    wb_ref,
    mid_ref,
    grad_ref,
    pin_ref,
    sum_ref,
    cell_ref,
    left_ref,
    right_ref,
    att_gain_ref,
    tri_gain_ref,
    sum_gain_ref,
    wtgate_ref,
    wtgate_t_ref,
    wtout_ref,
    wtout_t_ref,
    wt_edges_ref,
    wleft_ref,
    wright_ref,
    out_ref,
    mid_grad_ref,
    back_ref,
    coef_ref,
    total_ref,
    planes_ref,
    grad_send,
    grad_recv,
    left_send,
    left_recv,
    right_send,
    right_recv,
    send,
    recv,
):
    rows, length, channels = mid_ref.shape
    block = math.gcd(rows, 4)
    blocks = rows // block
    me, count, second = position()

    def grad_x(b):
        part = pl.ds(b * block, block)
        return Exchange(grad_send, grad_recv, send, recv, b, me, count, second, part=part)

    def right_x(b):
        part = pl.ds(b * block, block)
        return Exchange(
            right_send, right_recv, send, recv, blocks + b, me, count, second, part=part
        )

    left_x = Exchange(left_send, left_recv, send, recv, 2 * blocks, me, count, second)
    enter(me, count, second)

    def flat(ref, part):
        return ref[part].reshape(block * length, channels)

    def middle(b, carry):
        part = pl.ds(b * block, block)
        bias = []
        for r in range(block):
            band = band_ref[b * block + r].T
            term = band[:, 0:1] * wb_ref[0:1]
            for h in range(1, heads):
                term = term + band[:, h : h + 1] * wb_ref[h : h + 1]
            bias.append(term)
        bias = jnp.concatenate(bias, axis=0)
        unit, rstd = standardize(flat(mid_ref, part).astype(F32))
        mid_grad = flat(grad_ref, part).astype(F32) + norm_grad(
            unit, rstd, att_gain_ref[...], flat(ng_ref, part) + bias
        )
        unit, _ = standardize(flat(pin_ref, part).astype(F32))
        gate = jax.nn.sigmoid(dot((unit * tri_gain_ref[...]).astype(BF16), wtgate_ref[...]))
        unit, rstd = standardize(flat(sum_ref, part).astype(F32))
        tri_out = dot((unit * sum_gain_ref[...]).astype(BF16), wtout_ref[...])
        gated = mid_grad * gate
        summed = dot(gated.astype(BF16), wtout_t_ref[...])
        back = gated * tri_out * (1.0 - gate)
        mid_grad_ref[part] = mid_grad.reshape(block, length, channels)
        back_ref[part] = back.astype(BF16).reshape(block, length, channels)
        sum_grad = norm_grad(unit, rstd, sum_gain_ref[...], summed)
        for r in range(block):
            value = sum_grad[r * length : (r + 1) * length].T
            value = value.reshape(count, channels // count, length)
            grad_send[:, b * block + r] = value.astype(BF16)
        grad_x(b).start()
        return carry

    lax.fori_loop(0, blocks, middle, 0)

    def prepare(b, carry):
        part = pl.ds(b * block, block)
        unit, _ = standardize(flat(pin_ref, part).astype(F32))
        proj = dot_t(wt_edges_ref[...], (unit * tri_gain_ref[...]).astype(BF16))
        for r in range(block):
            cell = cell_ref[b * block + r]
            for side in range(2):
                p = proj[:, r * length : (r + 1) * length]
                p = p[2 * side * channels : 2 * (side + 1) * channels]
                s = jax.nn.sigmoid(p[:channels])
                gate = cell * s
                low = 2 * side * channels
                coef_ref[b * block + r, low : low + channels] = gate * p[channels:] * (1.0 - s)
                coef_ref[b * block + r, low + channels : low + 2 * channels] = gate
        return carry

    lax.fori_loop(0, blocks, prepare, 0)

    def take(b, carry):
        grad_x(b).wait()
        return carry

    lax.fori_loop(0, blocks, take, 0)
    to_planes(grad_recv, planes_ref)
    planes = planes_ref.shape[0]
    outs = [dot(planes_ref[c], right_ref[c]) for c in range(planes)]
    outs = jnp.swapaxes(jnp.stack(outs, axis=0), 0, 1)
    left_send[...] = outs.reshape(left_send.shape).astype(BF16)
    left_x.start()
    outs = [dot(planes_ref[c].astype(F32).T.astype(BF16), left_ref[c]) for c in range(planes)]
    outs = jnp.swapaxes(jnp.stack(outs, axis=0), 0, 1)
    right_send[...] = outs.reshape(right_send.shape).astype(BF16)

    def give(b, carry):
        right_x(b).start()
        return carry

    lax.fori_loop(0, blocks, give, 0)

    def edge_grad(received, w_ref, r, side):
        grad = received[:, r].astype(F32).reshape(channels, length)
        low = 2 * side * channels
        first = grad * coef_ref[r, low : low + channels]
        second_half = grad * coef_ref[r, low + channels : low + 2 * channels]
        both = jnp.concatenate([first, second_half], axis=0).astype(BF16)
        return dot(w_ref[...], both).T

    left_x.wait()

    def left_part(b, carry):
        part = pl.ds(b * block, block)
        gates = dot(flat(back_ref, part), wtgate_t_ref[...])
        for r in range(block):
            grad = edge_grad(left_recv, wleft_ref, b * block + r, 0)
            total_ref[b * block + r] = gates[r * length : (r + 1) * length] + grad
        return carry

    lax.fori_loop(0, blocks, left_part, 0)

    def finish(b, carry):
        right_x(b).wait()
        part = pl.ds(b * block, block)
        grads = [
            total_ref[b * block + r] + edge_grad(right_recv, wright_ref, b * block + r, 1)
            for r in range(block)
        ]
        unit, rstd = standardize(flat(pin_ref, part).astype(F32))
        total = jnp.concatenate(grads, axis=0)
        result = flat(mid_grad_ref, part) + norm_grad(unit, rstd, tri_gain_ref[...], total)
        out_ref[part] = result.reshape(block, length, channels)
        return carry

    lax.fori_loop(0, blocks, finish, 0)


def left_kernel(grad_ref, right_ref, out_ref):
    planes = grad_ref.shape[0]
    outs = []
    for c in range(planes):
        outs.append(dot(grad_ref[c], right_ref[c]))
    if planes % 8 == 0:
        out_ref[...] = jnp.swapaxes(jnp.stack(outs, axis=0), 0, 1).astype(BF16)
    else:
        for c in range(planes):
            out_ref[c] = outs[c].astype(BF16)


def right_kernel(grad_ref, left_ref, out_ref):
    planes = grad_ref.shape[0]
    outs = []
    for c in range(planes):
        outs.append(dot(grad_ref[c].T, left_ref[c]))
    if planes % 8 == 0:
        out_ref[...] = jnp.swapaxes(jnp.stack(outs, axis=0), 0, 1).astype(BF16)
    else:
        for c in range(planes):
            out_ref[c] = outs[c].astype(BF16)


def final_kernel(
    split,
    left_ref,
    right_ref,
    back_ref,
    mid_ref,
    pin_ref,
    cell_ref,
    gain_ref,
    wt_ref,
    wleft_ref,
    wright_ref,
    wtgate_t_ref,
    out_ref,
):
    block, length, channels = pin_ref.shape
    unit, rstd = standardize(rows_of(pin_ref).astype(F32))
    normed = (unit * gain_ref[...]).astype(BF16)
    proj = dot_t(wt_ref[...], normed)

    def backward(grad, part):
        s = jax.nn.sigmoid(part[:channels])
        gs = grad * s
        return jnp.concatenate([gs * part[channels:] * (1.0 - s), gs], axis=0).astype(BF16)

    grads = []
    for r in range(block):
        part = proj[:, r * length : (r + 1) * length]
        cell = cell_ref[r]
        left = backward(get_planes(left_ref, r, split) * cell, part[: 2 * channels])
        right = backward(get_planes(right_ref, r, split) * cell, part[2 * channels :])
        grads.append((dot(wleft_ref[...], left) + dot(wright_ref[...], right)).T)
    total = jnp.concatenate(grads, axis=0) + dot(rows_of(back_ref), wtgate_t_ref[...])
    result = rows_of(mid_ref) + norm_grad(unit, rstd, gain_ref[...], total)
    out_ref[...] = result.reshape(block, length, channels)


def whole(array):
    zeros = (0,) * array.ndim
    return pl.BlockSpec(array.shape, lambda i: zeros)


def banded(array, block):
    rest = array.shape[1:]
    zeros = (0,) * len(rest)
    return pl.BlockSpec((block,) + rest, lambda i: (i,) + zeros)


def params():
    return pltpu.CompilerParams(
        dimension_semantics=("arbitrary",), vmem_limit_bytes=VMEM_BYTES
    )


def per_device(
    pair_in,
    tri_sum,
    pair_mid,
    pair_grad,
    residue_mask,
    tri_gain,
    w_left,
    w_right,
    w_tgate,
    sum_gain,
    w_tout,
    att_gain,
    w_qkvg,
    w_bias,
    w_aout,
):
    rows, length, channels = pair_in.shape
    heads = w_bias.shape[1]
    devices = length // rows
    group = channels // devices
    split = group % 8 == 0
    block = math.gcd(rows, 4)
    key_mask = residue_mask.astype(F32)
    band_index = lax.axis_index(AXES)
    row_mask = lax.dynamic_slice_in_dim(key_mask, band_index * rows, rows)
    cell = (row_mask[:, None] * key_mask[None, :])[:, None, :]
    tri_gain, sum_gain, att_gain = tri_gain[None], sum_gain[None], att_gain[None]
    wt_edges = jnp.concatenate([w_left.T, w_right.T], axis=0)
    wt_qkvg = w_qkvg.T
    w_kv = w_qkvg[:, channels : 3 * channels]
    w_qg = jnp.concatenate([w_qkvg[:, :channels], w_qkvg[:, 3 * channels :]], axis=1)
    wt_kv = wt_qkvg[channels : 3 * channels]

    if split:
        plane_shape = jax.ShapeDtypeStruct((devices, rows, group, length), BF16)
        plane_spec = pl.BlockSpec((devices, block, group, length), lambda i: (0, i, 0, 0))
    else:
        plane_shape = jax.ShapeDtypeStruct((rows, channels, length), BF16)
        plane_spec = pl.BlockSpec((block, channels, length), lambda i: (i, 0, 0))

    def spread(planes):
        if not split:
            planes = jnp.swapaxes(planes.reshape(rows, devices, group, length), 0, 1)
        gathered = lax.all_to_all(planes, AXES, split_axis=0, concat_axis=0, tiled=True)
        return jnp.swapaxes(gathered.reshape(length, group, length), 0, 1)

    def collect(planes):
        if not split:
            planes = jnp.swapaxes(planes, 0, 1)
        planes = planes.reshape(devices, rows, group, length)
        back = lax.all_to_all(planes, AXES, split_axis=0, concat_axis=0, tiled=True)
        if not split:
            back = jnp.swapaxes(back, 0, 1).reshape(rows, channels, length)
        return back

    def run(kernel, args, banded_count, out_shape, out_specs, special=()):
        specs = [banded(a, block) for a in args[:banded_count]]
        specs += [whole(a) for a in args[banded_count:]]
        for position, spec in special:
            specs[position] = spec
        return pl.pallas_call(
            kernel,
            grid=(rows // block,),
            in_specs=specs,
            out_specs=out_specs,
            out_shape=out_shape,
            compiler_params=params(),
        )(*args)

    if split:
        operands = (
            pair_in,
            pair_mid,
            pair_grad,
            cell,
            jnp.where(residue_mask > 0, 0.0, -1e30)[None],
            tri_gain,
            att_gain,
            wt_edges,
            jnp.pad(w_bias.T, ((0, -heads % 16), (0, 0))),
            wt_qkvg,
            w_kv,
            w_qg,
            wt_kv,
            w_aout,
        )
        vmem = pl.BlockSpec(memory_space=pltpu.VMEM)
        planes = jax.ShapeDtypeStruct((group, length, length), BF16)
        ones = pltpu.VMEM((devices, rows, group, length), BF16)
        parts = pltpu.VMEM((devices, heads, rows, length), BF16)
        normed_grad, band, left_planes, right_planes = pl.pallas_call(
            functools.partial(first_kernel, heads),
            in_specs=[vmem] * len(operands),
            out_specs=[vmem] * 4,
            out_shape=(
                jax.ShapeDtypeStruct((rows, length, channels), F32),
                jax.ShapeDtypeStruct((heads, rows, length), F32),
                planes,
                planes,
            ),
            scratch_shapes=[
                pltpu.VMEM((rows, length, channels), BF16),
                pltpu.VMEM((heads, rows, length), BF16),
                parts,
                ones,
                ones,
                ones,
                ones,
                parts,
                parts,
                pltpu.VMEM((heads, length, length), F32),
                pltpu.VMEM((heads, channels, length), BF16),
                pltpu.VMEM((heads, channels, length), BF16),
                pltpu.VMEM((heads, length, length), F32),
                pltpu.SemaphoreType.DMA((4, devices)),
                pltpu.SemaphoreType.DMA((4, devices)),
            ],
            compiler_params=pltpu.CompilerParams(
                collective_id=0, has_side_effects=True, vmem_limit_bytes=VMEM_BYTES
            ),
        )(*operands)
        band = jnp.swapaxes(band, 0, 1)
    else:
        unit, _ = standardize(pair_mid.astype(F32))
        normed_mid = (unit * att_gain).astype(BF16)
        bias_local = lax.dot_general(
            w_bias, normed_mid, (((0,), (2,)), ((), ())), preferred_element_type=F32
        ).astype(BF16)
        bias_full = lax.all_gather(bias_local, AXES, axis=1, tiled=True)
        bias_t = jnp.swapaxes(bias_full, 1, 2).astype(F32) * math.log2(math.e)
        bias_t = bias_t + jnp.where(residue_mask > 0, 0.0, -1e30)[None, :, None]

        left_act, right_act = run(
            functools.partial(edge_kernel, split),
            (pair_in, cell, tri_gain, wt_edges),
            2,
            (plane_shape, plane_shape),
            (plane_spec, plane_spec),
        )
        left_planes, right_planes = spread(left_act), spread(right_act)

        attention_args = (
            pair_mid,
            pair_grad,
            att_gain,
            wt_qkvg,
            w_kv,
            w_qg,
            wt_kv,
            w_aout,
            bias_t,
        )
        normed_grad, bias_part = pl.pallas_call(
            functools.partial(attention_kernel, heads),
            grid=(rows,),
            in_specs=[banded(a, 1) for a in attention_args[:2]]
            + [whole(a) for a in attention_args[2:]],
            out_specs=(
                pl.BlockSpec((1, length, channels), lambda i: (i, 0, 0)),
                pl.BlockSpec((heads, length, length), lambda i: (0, 0, 0)),
            ),
            out_shape=(
                jax.ShapeDtypeStruct((rows, length, channels), F32),
                jax.ShapeDtypeStruct((heads, length, length), BF16),
            ),
            scratch_shapes=[
                pltpu.VMEM((heads, channels, length), BF16),
                pltpu.VMEM((heads, channels, length), BF16),
                pltpu.VMEM((heads, length, length), F32),
            ],
            compiler_params=params(),
            cost_estimate=pl.CostEstimate(
                flops=rows * heads * 12 * length * length * channels,
                bytes_accessed=rows * length * channels * 8,
                transcendentals=rows * heads * length * length,
            ),
        )(*attention_args)
        bias_part = jnp.swapaxes(bias_part.reshape(heads, devices, rows, length), 0, 1)
        bias_parts = lax.all_to_all(bias_part, AXES, split_axis=0, concat_axis=0, tiled=True)
        band = jnp.swapaxes(jnp.sum(bias_parts.astype(F32), axis=0), 0, 1)
    band = jnp.pad(band, ((0, 0), (0, -heads % 8), (0, 0)))

    row_spec = pl.BlockSpec((block, length, channels), lambda i: (i, 0, 0))
    row_shape = jax.ShapeDtypeStruct((rows, length, channels), F32)
    wb_t = jnp.pad(w_bias.astype(F32).T, ((0, -heads % 8), (0, 0)))
    if split:
        operands = (
            normed_grad,
            band,
            wb_t,
            pair_mid,
            pair_grad,
            pair_in,
            tri_sum,
            cell,
            left_planes,
            right_planes,
            att_gain,
            tri_gain,
            sum_gain,
            w_tgate,
            w_tgate.T,
            w_tout,
            w_tout.T,
            wt_edges,
            w_left,
            w_right,
        )
        return pl.pallas_call(
            functools.partial(second_kernel, heads),
            in_specs=[vmem] * len(operands),
            out_specs=vmem,
            out_shape=row_shape,
            scratch_shapes=[
                pltpu.VMEM((rows, length, channels), F32),
                pltpu.VMEM((rows, length, channels), BF16),
                pltpu.VMEM((rows, 4 * channels, length), F32),
                pltpu.VMEM((rows, length, channels), F32),
                pltpu.VMEM((group, length, length), BF16),
                ones,
                ones,
                ones,
                ones,
                ones,
                ones,
                pltpu.SemaphoreType.DMA((2 * (rows // block) + 1, devices)),
                pltpu.SemaphoreType.DMA((2 * (rows // block) + 1, devices)),
            ],
            compiler_params=pltpu.CompilerParams(
                collective_id=1, has_side_effects=True, vmem_limit_bytes=VMEM_BYTES
            ),
        )(*operands)
    mid_grad, gate_back, sum_grad = pl.pallas_call(
        functools.partial(middle_kernel, split, heads),
        grid=(rows // block,),
        in_specs=[banded(normed_grad, block), banded(band, block), whole(wb_t)]
        + [row_spec] * 4
        + [whole(a) for a in (att_gain, tri_gain, sum_gain, w_tgate, w_tout, w_tout)],
        out_specs=(row_spec, row_spec, plane_spec),
        out_shape=(row_shape, jax.ShapeDtypeStruct(row_shape.shape, BF16), plane_shape),
        compiler_params=params(),
    )(
        normed_grad,
        band,
        wb_t,
        pair_mid,
        pair_grad,
        pair_in,
        tri_sum,
        att_gain,
        tri_gain,
        sum_gain,
        w_tgate,
        w_tout,
        w_tout.T,
    )
    grad_planes = spread(sum_grad)

    def product(kernel, other):
        shape = (length, group, length) if split else (group, length, length)
        return pl.pallas_call(
            kernel,
            in_specs=[pl.BlockSpec(memory_space=pltpu.VMEM)] * 2,
            out_specs=pl.BlockSpec(memory_space=pltpu.VMEM),
            out_shape=jax.ShapeDtypeStruct(shape, BF16),
            compiler_params=pltpu.CompilerParams(vmem_limit_bytes=VMEM_BYTES),
        )(grad_planes, other)

    left_grad = collect(product(left_kernel, right_planes))
    right_grad = collect(product(right_kernel, left_planes))
    return run(
        functools.partial(final_kernel, split),
        (
            left_grad,
            right_grad,
            gate_back,
            mid_grad,
            pair_in,
            cell,
            tri_gain,
            wt_edges,
            w_left,
            w_right,
            w_tgate.T,
        ),
        6,
        row_shape,
        row_spec,
        special=((0, plane_spec), (1, plane_spec)),
    )


def solution(mesh):
    rows = P(("crop", "ia", "ja"), None, None)
    placed = (rows, rows, rows, rows, P("crop")) + (P(),) * 10
    return jax.shard_map(
        per_device, mesh=mesh, in_specs=placed, out_specs=rows, check_vma=False
    )
```

```python
import functools
import math

import jax
import jax.numpy as jnp
from jax import lax
from jax.experimental import pallas as pl
from jax.experimental.pallas import tpu as pltpu
from jax.sharding import PartitionSpec as P

EPSILON = 1e-05
F32 = jnp.float32
BF16 = jnp.bfloat16
VMEM_BYTES = 48 * 1024 * 1024
AXES = ("ia", "ja")


def dot(a, b):
    return jnp.dot(a, b, preferred_element_type=F32)


def dot_t(a, b):
    return lax.dot_general(a, b, (((1,), (1,)), ((), ())), preferred_element_type=F32)


def standardize(v):
    average = jnp.mean(v, axis=-1, keepdims=True)
    centred = v - average
    second = jnp.mean(centred * centred, axis=-1, keepdims=True)
    rstd = lax.rsqrt(second + EPSILON)
    return centred * rstd, rstd


def norm_grad(unit, rstd, gain, cotangent):
    g = cotangent * gain
    return rstd * (
        g
        - jnp.mean(g, axis=-1, keepdims=True)
        - unit * jnp.mean(g * unit, axis=-1, keepdims=True)
    )


def rows_of(ref):
    block = ref[...]
    return block.reshape(block.shape[0] * block.shape[1], block.shape[2])


def put_planes(ref, r, value, split):
    if split:
        ref[:, r] = value.reshape(ref.shape[0], ref.shape[2], ref.shape[3]).astype(BF16)
    else:
        ref[r] = value.astype(BF16)


def get_planes(ref, r, split):
    if split:
        value = ref[:, r].astype(F32)
        return value.reshape(value.shape[0] * value.shape[1], value.shape[2])
    return ref[r].astype(F32)


def edge_kernel(split, pin_ref, cell_ref, gain_ref, wt_ref, left_ref, right_ref):
    block, length, channels = pin_ref.shape
    unit, _ = standardize(rows_of(pin_ref).astype(F32))
    normed = (unit * gain_ref[...]).astype(BF16)
    proj = dot_t(wt_ref[...], normed)
    for r in range(block):
        part = proj[:, r * length : (r + 1) * length]
        cell = cell_ref[r]
        left = cell * jax.nn.sigmoid(part[:channels]) * part[channels : 2 * channels]
        right = (
            cell * jax.nn.sigmoid(part[2 * channels : 3 * channels]) * part[3 * channels :]
        )
        put_planes(left_ref, r, left, split)
        put_planes(right_ref, r, right, split)


def attention_row(
    heads, normed, grad_row, wt_ref, wkv_ref, wqg_ref, wtkv_ref, waout_ref, bias_ref, q_block, o_block, acc
):
    length, channels = normed.shape
    dim = channels // heads
    scale = dim ** (-0.5)
    proj = dot_t(wt_ref[...], normed)
    kv = dot(normed, wkv_ref[...]).astype(BF16)
    keys, values = kv[:, :channels], kv[:, channels:]
    keys_t = proj[channels : 2 * channels].astype(BF16)
    values_t = proj[2 * channels : 3 * channels].astype(BF16)
    queries_t = proj[:channels].astype(BF16)
    gate = jax.nn.sigmoid(proj[3 * channels :])
    gated = dot_t(waout_ref[...], grad_row)
    out_t = (gated * gate).astype(BF16)
    for h in range(heads):
        rows = slice(h * dim, (h + 1) * dim)
        q_block[h, rows] = queries_t[rows]
        o_block[h, rows] = out_t[rows]
    attended, query_grads = [], []
    key_grad = jnp.zeros((length, channels), F32)
    value_grad = jnp.zeros((length, channels), F32)
    for h in range(heads):
        rows = slice(h * dim, (h + 1) * dim)
        scores = dot(keys, q_block[h])
        e = jnp.exp2(scores * (scale * math.log2(math.e)) + bias_ref[h])
        probs = e * (1.0 / jnp.sum(e, axis=0, keepdims=True))
        probs_b = probs.astype(BF16)
        prob_grad = dot(values, o_block[h])
        weighted = probs * prob_grad
        score_grad = weighted - probs * jnp.sum(weighted, axis=0, keepdims=True)
        score_b = score_grad.astype(BF16)
        acc[h] += score_grad
        attended.append(dot(values_t[rows], probs_b))
        query_grads.append(dot(keys_t[rows], score_b))
        key_grad += dot_t(score_b, q_block[h])
        value_grad += dot_t(probs_b, o_block[h])
    attended = jnp.concatenate(attended, axis=0)
    query_grad = jnp.concatenate(query_grads, axis=0) * scale
    logit_grad = gated * attended * gate * (1.0 - gate)
    qg = jnp.concatenate([query_grad, logit_grad], axis=0).astype(BF16)
    kv_grad = jnp.concatenate([key_grad * scale, value_grad], axis=1).astype(BF16)
    return dot(kv_grad, wtkv_ref[...]) + dot(wqg_ref[...], qg).T


def attention_kernel(
    heads,
    mid_ref,
    grad_ref,
    gain_ref,
    wt_ref,
    wkv_ref,
    wqg_ref,
    wtkv_ref,
    waout_ref,
    bias_ref,
    out_ref,
    bias_out_ref,
    q_block,
    o_block,
    acc,
):
    step = pl.program_id(0)

    @pl.when(step == 0)
    def _():
        q_block[...] = jnp.zeros_like(q_block)
        o_block[...] = jnp.zeros_like(o_block)
        acc[...] = jnp.zeros_like(acc)

    unit, _ = standardize(mid_ref[0].astype(F32))
    normed = (unit * gain_ref[...]).astype(BF16)
    out_ref[0] = attention_row(
        heads, normed, grad_ref[0], wt_ref, wkv_ref, wqg_ref, wtkv_ref, waout_ref, bias_ref, q_block, o_block, acc
    )

    @pl.when(step == pl.num_programs(0) - 1)
    def _():
        for h in range(heads):
            bias_out_ref[h] = acc[h].T.astype(BF16)


def enter(me, count, second):
    barrier = pltpu.get_barrier_semaphore()

    def greet(p, carry):
        other = lax.rem(me + p, count)
        pl.semaphore_signal(
            barrier, inc=1, device_id=place(other, second), device_id_type=pl.DeviceIdType.MESH
        )
        return carry

    lax.fori_loop(1, count, greet, 0)
    pl.semaphore_wait(barrier, count - 1)


def place(index, second):
    return {"ia": lax.div(index, second), "ja": lax.rem(index, second)}


class Exchange:
    def __init__(self, source, target, send, recv, slot, me, count, second, same=False, part=None):
        self.source, self.target, self.same, self.part = source, target, same, part
        self.send, self.recv, self.slot = send, recv, slot
        self.me, self.count, self.second = me, count, second

    def copy(self, p):
        other = lax.rem(self.me + p, self.count)
        source = self.source if self.same else self.source.at[other]
        target = self.target.at[self.me]
        if self.part is not None:
            source, target = source.at[self.part], target.at[self.part]
        return pltpu.make_async_remote_copy(
            src_ref=source,
            dst_ref=target,
            send_sem=self.send.at[self.slot, p],
            recv_sem=self.recv.at[self.slot, p],
            device_id=place(other, self.second),
            device_id_type=pl.DeviceIdType.MESH,
        )

    def start(self):
        def go(p, carry):
            self.copy(p).start()
            return carry

        lax.fori_loop(1, self.count, go, 0)
        if self.same:
            self.target[self.me] = self.source[...]
        elif self.part is not None:
            self.target[self.me, self.part] = self.source[self.me, self.part]
        else:
            self.target[self.me] = self.source[self.me]

    def wait(self):
        def go(p, carry):
            self.copy(p).wait()
            return carry

        lax.fori_loop(1, self.count, go, 0)


def position():
    second = lax.axis_size("ja")
    return (
        lax.axis_index("ia") * second + lax.axis_index("ja"),
        lax.axis_size("ia") * second,
        second,
    )


def first_kernel(
    heads,
    in_ref,
    mid_ref,
    grad_ref,
    cell_ref,
    mask_ref,
    tri_gain_ref,
    att_gain_ref,
    w_left_ref,
    w_right_ref,
    w_bias_ref,
    w_ref,
    waout_ref,
    out_ref,
    band_ref,
    left_out_ref,
    right_out_ref,
    normed_ref,
    bias_send,
    bias_recv,
    left_send,
    left_recv,
    right_send,
    right_recv,
    part_send,
    part_recv,
    bias_ref,
    q_block,
    o_block,
    acc,
    wt_edges_ref,
    wide_ref,
    wt_ref,
    wkv_ref,
    wqg_ref,
    wtkv_ref,
    send,
    recv,
):
    rows, length, channels = in_ref.shape
    block = math.gcd(rows, 4)
    me, count, second = position()
    link = (send, recv)
    bias_x = Exchange(bias_send, bias_recv, *link, 0, me, count, second, same=True)
    left_x = Exchange(left_send, left_recv, *link, 1, me, count, second)
    right_x = Exchange(right_send, right_recv, *link, 2, me, count, second)
    part_x = Exchange(part_send, part_recv, *link, 3, me, count, second)

    wide_ref[...] = jnp.zeros_like(wide_ref)
    wide_ref[:, :heads] = w_bias_ref[...].astype(F32)
    w_bias_t = wide_ref[...].T[:16].astype(BF16)
    bias_rows = []
    for b in range(rows // block):
        part = slice(b * block, (b + 1) * block)
        unit, _ = standardize(mid_ref[part].reshape(block * length, channels).astype(F32))
        normed = (unit * att_gain_ref[...]).astype(BF16)
        normed_ref[part] = normed.reshape(block, length, channels)
        bias = dot_t(w_bias_t, normed)
        bias_rows += [bias[:, r * length : (r + 1) * length] for r in range(block)]
    for h in range(heads):
        bias_send[h] = jnp.concatenate([b[h : h + 1] for b in bias_rows], axis=0).astype(BF16)
    enter(me, count, second)
    bias_x.start()
    transposed_edges(w_left_ref, w_right_ref, wt_edges_ref)
    wt_ref[...] = w_ref[...].astype(F32).T.astype(BF16)
    wkv_ref[...] = w_ref[:, channels : 3 * channels]
    wqg_ref[:, :channels] = w_ref[:, :channels]
    wqg_ref[:, channels:] = w_ref[:, 3 * channels :]
    wtkv_ref[...] = wt_ref[channels : 3 * channels]

    def edges(b, carry):
        part = pl.ds(b * block, block)
        unit, _ = standardize(in_ref[part].reshape(block * length, channels).astype(F32))
        proj = dot_t(wt_edges_ref[...], (unit * tri_gain_ref[...]).astype(BF16))
        for r in range(block):
            p = proj[:, r * length : (r + 1) * length]
            cell = cell_ref[b * block + r]
            left = cell * jax.nn.sigmoid(p[:channels]) * p[channels : 2 * channels]
            right = cell * jax.nn.sigmoid(p[2 * channels : 3 * channels]) * p[3 * channels :]
            shape = (count, channels // count, length)
            left_send[:, b * block + r] = left.reshape(shape).astype(BF16)
            right_send[:, b * block + r] = right.reshape(shape).astype(BF16)
        return carry

    lax.fori_loop(0, rows // block, edges, 0)
    bias_x.wait()
    left_x.start()
    right_x.start()
    q_block[...] = jnp.zeros_like(q_block)
    o_block[...] = jnp.zeros_like(o_block)
    acc[...] = jnp.zeros_like(acc)
    for h in range(heads):
        full = bias_recv[:, h].astype(F32).reshape(length, length)
        bias_ref[h] = (full * math.log2(math.e) + mask_ref[...]).T

    def attend(i, carry):
        out_ref[i] = attention_row(
            heads,
            normed_ref[i],
            grad_ref[i],
            wt_ref,
            wkv_ref,
            wqg_ref,
            wtkv_ref,
            waout_ref,
            bias_ref,
            q_block,
            o_block,
            acc,
        )
        return carry

    lax.fori_loop(0, rows, attend, 0)
    for h in range(heads):
        part_send[:, h] = acc[h].T.reshape(count, rows, length).astype(BF16)
    part_x.start()
    left_x.wait()
    to_planes(left_recv, left_out_ref)
    right_x.wait()
    to_planes(right_recv, right_out_ref)
    part_x.wait()
    for h in range(heads):
        band_ref[h] = jnp.sum(part_recv[:, h].astype(F32), axis=0)


def transposed_edges(w_left_ref, w_right_ref, out_ref):
    half = w_left_ref.shape[1]
    out_ref[:half] = w_left_ref[...].astype(F32).T.astype(BF16)
    out_ref[half:] = w_right_ref[...].astype(F32).T.astype(BF16)


def to_planes(received, planes_ref):
    count, rows = received.shape[:2]

    def move(s, carry):
        value = jnp.swapaxes(received[s].astype(F32), 0, 1).astype(BF16)
        planes_ref[:, pl.ds(pl.multiple_of(s * rows, rows), rows), :] = value
        return carry

    lax.fori_loop(0, count, move, 0)


def middle_kernel(
    split,
    heads,
    ng_ref,
    band_ref,
    wb_ref,
    mid_ref,
    grad_ref,
    pin_ref,
    sum_ref,
    att_gain_ref,
    tri_gain_ref,
    sum_gain_ref,
    wtgate_ref,
    wtout_ref,
    wtout_t_ref,
    mid_out_ref,
    back_ref,
    planes_ref,
):
    block, length, channels = mid_ref.shape
    bias = []
    for r in range(block):
        band = band_ref[r].T
        part = band[:, 0:1] * wb_ref[0:1]
        for h in range(1, heads):
            part = part + band[:, h : h + 1] * wb_ref[h : h + 1]
        bias.append(part)
    bias = jnp.concatenate(bias, axis=0)
    unit, rstd = standardize(rows_of(mid_ref).astype(F32))
    mid_grad = rows_of(grad_ref).astype(F32) + norm_grad(
        unit, rstd, att_gain_ref[...], rows_of(ng_ref) + bias
    )
    unit, _ = standardize(rows_of(pin_ref).astype(F32))
    gate = jax.nn.sigmoid(dot((unit * tri_gain_ref[...]).astype(BF16), wtgate_ref[...]))
    unit, rstd = standardize(rows_of(sum_ref).astype(F32))
    tri_out = dot((unit * sum_gain_ref[...]).astype(BF16), wtout_ref[...])
    gated = mid_grad * gate
    summed = dot(gated.astype(BF16), wtout_t_ref[...])
    back = gated * tri_out * (1.0 - gate)
    mid_out_ref[...] = mid_grad.reshape(block, length, channels)
    back_ref[...] = back.astype(BF16).reshape(block, length, channels)
    sum_grad = norm_grad(unit, rstd, sum_gain_ref[...], summed)
    for r in range(block):
        put_planes(planes_ref, r, sum_grad[r * length : (r + 1) * length].T, split)


def second_kernel(
    heads,
    ng_ref,
    band_ref,
    w_bias_ref,
    mid_ref,
    grad_ref,
    pin_ref,
    sum_ref,
    cell_ref,
    left_ref,
    right_ref,
    att_gain_ref,
    tri_gain_ref,
    sum_gain_ref,
    wtgate_ref,
    wtout_ref,
    wleft_ref,
    wright_ref,
    out_ref,
    mid_grad_ref,
    back_ref,
    coef_ref,
    total_ref,
    planes_ref,
    grad_send,
    grad_recv,
    left_send,
    left_recv,
    right_send,
    right_recv,
    wt_edges_ref,
    wide_ref,
    wb_ref,
    send,
    recv,
):
    rows, length, channels = mid_ref.shape
    block = math.gcd(rows, 4)
    blocks = rows // block
    me, count, second = position()

    def grad_x(b):
        part = pl.ds(b * block, block)
        return Exchange(grad_send, grad_recv, send, recv, b, me, count, second, part=part)

    def right_x(b):
        part = pl.ds(b * block, block)
        return Exchange(
            right_send, right_recv, send, recv, blocks + b, me, count, second, part=part
        )

    left_x = Exchange(left_send, left_recv, send, recv, 2 * blocks, me, count, second)
    wide_ref[...] = jnp.zeros_like(wide_ref)
    wide_ref[:, :heads] = w_bias_ref[...].astype(F32)
    wb_ref[...] = wide_ref[...].T
    enter(me, count, second)

    def flat(ref, part):
        return ref[part].reshape(block * length, channels)

    def middle(b, carry):
        part = pl.ds(b * block, block)
        bias = []
        for r in range(block):
            band = band_ref[b * block + r].T
            term = band[:, 0:1] * wb_ref[0:1]
            for h in range(1, heads):
                term = term + band[:, h : h + 1] * wb_ref[h : h + 1]
            bias.append(term)
        bias = jnp.concatenate(bias, axis=0)
        unit, rstd = standardize(flat(mid_ref, part).astype(F32))
        mid_grad = flat(grad_ref, part).astype(F32) + norm_grad(
            unit, rstd, att_gain_ref[...], flat(ng_ref, part) + bias
        )
        unit, _ = standardize(flat(pin_ref, part).astype(F32))
        gate = jax.nn.sigmoid(dot((unit * tri_gain_ref[...]).astype(BF16), wtgate_ref[...]))
        unit, rstd = standardize(flat(sum_ref, part).astype(F32))
        tri_out = dot((unit * sum_gain_ref[...]).astype(BF16), wtout_ref[...])
        gated = mid_grad * gate
        summed = dot_t(gated.astype(BF16), wtout_ref[...])
        back = gated * tri_out * (1.0 - gate)
        mid_grad_ref[part] = mid_grad.reshape(block, length, channels)
        back_ref[part] = back.astype(BF16).reshape(block, length, channels)
        sum_grad = norm_grad(unit, rstd, sum_gain_ref[...], summed)
        for r in range(block):
            value = sum_grad[r * length : (r + 1) * length].T
            value = value.reshape(count, channels // count, length)
            grad_send[:, b * block + r] = value.astype(BF16)
        grad_x(b).start()
        return carry

    lax.fori_loop(0, blocks, middle, 0)
    transposed_edges(wleft_ref, wright_ref, wt_edges_ref)

    def prepare(b, carry):
        part = pl.ds(b * block, block)
        unit, _ = standardize(flat(pin_ref, part).astype(F32))
        proj = dot_t(wt_edges_ref[...], (unit * tri_gain_ref[...]).astype(BF16))
        for r in range(block):
            cell = cell_ref[b * block + r]
            for side in range(2):
                p = proj[:, r * length : (r + 1) * length]
                p = p[2 * side * channels : 2 * (side + 1) * channels]
                s = jax.nn.sigmoid(p[:channels])
                gate = cell * s
                low = 2 * side * channels
                coef_ref[b * block + r, low : low + channels] = gate * p[channels:] * (1.0 - s)
                coef_ref[b * block + r, low + channels : low + 2 * channels] = gate
        return carry

    lax.fori_loop(0, blocks, prepare, 0)

    def take(b, carry):
        grad_x(b).wait()
        return carry

    lax.fori_loop(0, blocks, take, 0)
    to_planes(grad_recv, planes_ref)
    planes = planes_ref.shape[0]
    outs = [dot(planes_ref[c], right_ref[c]) for c in range(planes)]
    outs = jnp.swapaxes(jnp.stack(outs, axis=0), 0, 1)
    left_send[...] = outs.reshape(left_send.shape).astype(BF16)
    left_x.start()
    outs = [dot(planes_ref[c].astype(F32).T.astype(BF16), left_ref[c]) for c in range(planes)]
    outs = jnp.swapaxes(jnp.stack(outs, axis=0), 0, 1)
    right_send[...] = outs.reshape(right_send.shape).astype(BF16)

    def give(b, carry):
        right_x(b).start()
        return carry

    lax.fori_loop(0, blocks, give, 0)

    def edge_grad(received, w_ref, r, side):
        grad = received[:, r].astype(F32).reshape(channels, length)
        low = 2 * side * channels
        first = grad * coef_ref[r, low : low + channels]
        second_half = grad * coef_ref[r, low + channels : low + 2 * channels]
        both = jnp.concatenate([first, second_half], axis=0).astype(BF16)
        return dot(w_ref[...], both).T

    left_x.wait()

    def left_part(b, carry):
        part = pl.ds(b * block, block)
        gates = dot_t(flat(back_ref, part), wtgate_ref[...])
        for r in range(block):
            grad = edge_grad(left_recv, wleft_ref, b * block + r, 0)
            total_ref[b * block + r] = gates[r * length : (r + 1) * length] + grad
        return carry

    lax.fori_loop(0, blocks, left_part, 0)

    def finish(b, carry):
        right_x(b).wait()
        part = pl.ds(b * block, block)
        grads = [
            total_ref[b * block + r] + edge_grad(right_recv, wright_ref, b * block + r, 1)
            for r in range(block)
        ]
        unit, rstd = standardize(flat(pin_ref, part).astype(F32))
        total = jnp.concatenate(grads, axis=0)
        result = flat(mid_grad_ref, part) + norm_grad(unit, rstd, tri_gain_ref[...], total)
        out_ref[part] = result.reshape(block, length, channels)
        return carry

    lax.fori_loop(0, blocks, finish, 0)


def left_kernel(grad_ref, right_ref, out_ref):
    planes = grad_ref.shape[0]
    outs = []
    for c in range(planes):
        outs.append(dot(grad_ref[c], right_ref[c]))
    if planes % 8 == 0:
        out_ref[...] = jnp.swapaxes(jnp.stack(outs, axis=0), 0, 1).astype(BF16)
    else:
        for c in range(planes):
            out_ref[c] = outs[c].astype(BF16)


def right_kernel(grad_ref, left_ref, out_ref):
    planes = grad_ref.shape[0]
    outs = []
    for c in range(planes):
        outs.append(dot(grad_ref[c].T, left_ref[c]))
    if planes % 8 == 0:
        out_ref[...] = jnp.swapaxes(jnp.stack(outs, axis=0), 0, 1).astype(BF16)
    else:
        for c in range(planes):
            out_ref[c] = outs[c].astype(BF16)


def final_kernel(
    split,
    left_ref,
    right_ref,
    back_ref,
    mid_ref,
    pin_ref,
    cell_ref,
    gain_ref,
    wt_ref,
    wleft_ref,
    wright_ref,
    wtgate_t_ref,
    out_ref,
):
    block, length, channels = pin_ref.shape
    unit, rstd = standardize(rows_of(pin_ref).astype(F32))
    normed = (unit * gain_ref[...]).astype(BF16)
    proj = dot_t(wt_ref[...], normed)

    def backward(grad, part):
        s = jax.nn.sigmoid(part[:channels])
        gs = grad * s
        return jnp.concatenate([gs * part[channels:] * (1.0 - s), gs], axis=0).astype(BF16)

    grads = []
    for r in range(block):
        part = proj[:, r * length : (r + 1) * length]
        cell = cell_ref[r]
        left = backward(get_planes(left_ref, r, split) * cell, part[: 2 * channels])
        right = backward(get_planes(right_ref, r, split) * cell, part[2 * channels :])
        grads.append((dot(wleft_ref[...], left) + dot(wright_ref[...], right)).T)
    total = jnp.concatenate(grads, axis=0) + dot(rows_of(back_ref), wtgate_t_ref[...])
    result = rows_of(mid_ref) + norm_grad(unit, rstd, gain_ref[...], total)
    out_ref[...] = result.reshape(block, length, channels)


def whole(array):
    zeros = (0,) * array.ndim
    return pl.BlockSpec(array.shape, lambda i: zeros)


def banded(array, block):
    rest = array.shape[1:]
    zeros = (0,) * len(rest)
    return pl.BlockSpec((block,) + rest, lambda i: (i,) + zeros)


def params():
    return pltpu.CompilerParams(
        dimension_semantics=("arbitrary",), vmem_limit_bytes=VMEM_BYTES
    )


def per_device(
    pair_in,
    tri_sum,
    pair_mid,
    pair_grad,
    residue_mask,
    tri_gain,
    w_left,
    w_right,
    w_tgate,
    sum_gain,
    w_tout,
    att_gain,
    w_qkvg,
    w_bias,
    w_aout,
):
    rows, length, channels = pair_in.shape
    heads = w_bias.shape[1]
    devices = length // rows
    group = channels // devices
    split = group % 8 == 0
    block = math.gcd(rows, 4)
    key_mask = residue_mask.astype(F32)
    band_index = lax.axis_index(AXES)
    row_mask = lax.dynamic_slice_in_dim(key_mask, band_index * rows, rows)
    cell = (row_mask[:, None] * key_mask[None, :])[:, None, :]
    tri_gain, sum_gain, att_gain = tri_gain[None], sum_gain[None], att_gain[None]
    wt_edges = jnp.concatenate([w_left.T, w_right.T], axis=0)
    wt_qkvg = w_qkvg.T
    w_kv = w_qkvg[:, channels : 3 * channels]
    w_qg = jnp.concatenate([w_qkvg[:, :channels], w_qkvg[:, 3 * channels :]], axis=1)
    wt_kv = wt_qkvg[channels : 3 * channels]

    if split:
        plane_shape = jax.ShapeDtypeStruct((devices, rows, group, length), BF16)
        plane_spec = pl.BlockSpec((devices, block, group, length), lambda i: (0, i, 0, 0))
    else:
        plane_shape = jax.ShapeDtypeStruct((rows, channels, length), BF16)
        plane_spec = pl.BlockSpec((block, channels, length), lambda i: (i, 0, 0))

    def spread(planes):
        if not split:
            planes = jnp.swapaxes(planes.reshape(rows, devices, group, length), 0, 1)
        gathered = lax.all_to_all(planes, AXES, split_axis=0, concat_axis=0, tiled=True)
        return jnp.swapaxes(gathered.reshape(length, group, length), 0, 1)

    def collect(planes):
        if not split:
            planes = jnp.swapaxes(planes, 0, 1)
        planes = planes.reshape(devices, rows, group, length)
        back = lax.all_to_all(planes, AXES, split_axis=0, concat_axis=0, tiled=True)
        if not split:
            back = jnp.swapaxes(back, 0, 1).reshape(rows, channels, length)
        return back

    def run(kernel, args, banded_count, out_shape, out_specs, special=()):
        specs = [banded(a, block) for a in args[:banded_count]]
        specs += [whole(a) for a in args[banded_count:]]
        for position, spec in special:
            specs[position] = spec
        return pl.pallas_call(
            kernel,
            grid=(rows // block,),
            in_specs=specs,
            out_specs=out_specs,
            out_shape=out_shape,
            compiler_params=params(),
        )(*args)

    if split:
        operands = (
            pair_in,
            pair_mid,
            pair_grad,
            cell,
            jnp.where(residue_mask > 0, 0.0, -1e30)[None],
            tri_gain,
            att_gain,
            w_left,
            w_right,
            w_bias,
            w_qkvg,
            w_aout,
        )
        vmem = pl.BlockSpec(memory_space=pltpu.VMEM)
        planes = jax.ShapeDtypeStruct((group, length, length), BF16)
        ones = pltpu.VMEM((devices, rows, group, length), BF16)
        parts = pltpu.VMEM((devices, heads, rows, length), BF16)
        normed_grad, band, left_planes, right_planes = pl.pallas_call(
            functools.partial(first_kernel, heads),
            in_specs=[vmem] * len(operands),
            out_specs=[vmem] * 4,
            out_shape=(
                jax.ShapeDtypeStruct((rows, length, channels), F32),
                jax.ShapeDtypeStruct((heads, rows, length), F32),
                planes,
                planes,
            ),
            scratch_shapes=[
                pltpu.VMEM((rows, length, channels), BF16),
                pltpu.VMEM((heads, rows, length), BF16),
                parts,
                ones,
                ones,
                ones,
                ones,
                parts,
                parts,
                pltpu.VMEM((heads, length, length), F32),
                pltpu.VMEM((heads, channels, length), BF16),
                pltpu.VMEM((heads, channels, length), BF16),
                pltpu.VMEM((heads, length, length), F32),
                pltpu.VMEM((4 * channels, channels), BF16),
                pltpu.VMEM((channels, channels), F32),
                pltpu.VMEM((4 * channels, channels), BF16),
                pltpu.VMEM((channels, 2 * channels), BF16),
                pltpu.VMEM((channels, 2 * channels), BF16),
                pltpu.VMEM((2 * channels, channels), BF16),
                pltpu.SemaphoreType.DMA((4, devices)),
                pltpu.SemaphoreType.DMA((4, devices)),
            ],
            compiler_params=pltpu.CompilerParams(
                collective_id=0, has_side_effects=True, vmem_limit_bytes=VMEM_BYTES
            ),
        )(*operands)
        band = jnp.swapaxes(band, 0, 1)
    else:
        unit, _ = standardize(pair_mid.astype(F32))
        normed_mid = (unit * att_gain).astype(BF16)
        bias_local = lax.dot_general(
            w_bias, normed_mid, (((0,), (2,)), ((), ())), preferred_element_type=F32
        ).astype(BF16)
        bias_full = lax.all_gather(bias_local, AXES, axis=1, tiled=True)
        bias_t = jnp.swapaxes(bias_full, 1, 2).astype(F32) * math.log2(math.e)
        bias_t = bias_t + jnp.where(residue_mask > 0, 0.0, -1e30)[None, :, None]

        left_act, right_act = run(
            functools.partial(edge_kernel, split),
            (pair_in, cell, tri_gain, wt_edges),
            2,
            (plane_shape, plane_shape),
            (plane_spec, plane_spec),
        )
        left_planes, right_planes = spread(left_act), spread(right_act)

        attention_args = (
            pair_mid,
            pair_grad,
            att_gain,
            wt_qkvg,
            w_kv,
            w_qg,
            wt_kv,
            w_aout,
            bias_t,
        )
        normed_grad, bias_part = pl.pallas_call(
            functools.partial(attention_kernel, heads),
            grid=(rows,),
            in_specs=[banded(a, 1) for a in attention_args[:2]]
            + [whole(a) for a in attention_args[2:]],
            out_specs=(
                pl.BlockSpec((1, length, channels), lambda i: (i, 0, 0)),
                pl.BlockSpec((heads, length, length), lambda i: (0, 0, 0)),
            ),
            out_shape=(
                jax.ShapeDtypeStruct((rows, length, channels), F32),
                jax.ShapeDtypeStruct((heads, length, length), BF16),
            ),
            scratch_shapes=[
                pltpu.VMEM((heads, channels, length), BF16),
                pltpu.VMEM((heads, channels, length), BF16),
                pltpu.VMEM((heads, length, length), F32),
            ],
            compiler_params=params(),
            cost_estimate=pl.CostEstimate(
                flops=rows * heads * 12 * length * length * channels,
                bytes_accessed=rows * length * channels * 8,
                transcendentals=rows * heads * length * length,
            ),
        )(*attention_args)
        bias_part = jnp.swapaxes(bias_part.reshape(heads, devices, rows, length), 0, 1)
        bias_parts = lax.all_to_all(bias_part, AXES, split_axis=0, concat_axis=0, tiled=True)
        band = jnp.swapaxes(jnp.sum(bias_parts.astype(F32), axis=0), 0, 1)
    band = jnp.pad(band, ((0, 0), (0, -heads % 8), (0, 0)))

    row_spec = pl.BlockSpec((block, length, channels), lambda i: (i, 0, 0))
    row_shape = jax.ShapeDtypeStruct((rows, length, channels), F32)
    wb_t = jnp.pad(w_bias.astype(F32).T, ((0, -heads % 8), (0, 0)))
    if split:
        operands = (
            normed_grad,
            band,
            w_bias,
            pair_mid,
            pair_grad,
            pair_in,
            tri_sum,
            cell,
            left_planes,
            right_planes,
            att_gain,
            tri_gain,
            sum_gain,
            w_tgate,
            w_tout,
            w_left,
            w_right,
        )
        return pl.pallas_call(
            functools.partial(second_kernel, heads),
            in_specs=[vmem] * len(operands),
            out_specs=vmem,
            out_shape=row_shape,
            scratch_shapes=[
                pltpu.VMEM((rows, length, channels), F32),
                pltpu.VMEM((rows, length, channels), BF16),
                pltpu.VMEM((rows, 4 * channels, length), F32),
                pltpu.VMEM((rows, length, channels), F32),
                pltpu.VMEM((group, length, length), BF16),
                ones,
                ones,
                ones,
                ones,
                ones,
                ones,
                pltpu.VMEM((4 * channels, channels), BF16),
                pltpu.VMEM((channels, channels), F32),
                pltpu.VMEM((channels, channels), F32),
                pltpu.SemaphoreType.DMA((2 * (rows // block) + 1, devices)),
                pltpu.SemaphoreType.DMA((2 * (rows // block) + 1, devices)),
            ],
            compiler_params=pltpu.CompilerParams(
                collective_id=1, has_side_effects=True, vmem_limit_bytes=VMEM_BYTES
            ),
        )(*operands)
    mid_grad, gate_back, sum_grad = pl.pallas_call(
        functools.partial(middle_kernel, split, heads),
        grid=(rows // block,),
        in_specs=[banded(normed_grad, block), banded(band, block), whole(wb_t)]
        + [row_spec] * 4
        + [whole(a) for a in (att_gain, tri_gain, sum_gain, w_tgate, w_tout, w_tout)],
        out_specs=(row_spec, row_spec, plane_spec),
        out_shape=(row_shape, jax.ShapeDtypeStruct(row_shape.shape, BF16), plane_shape),
        compiler_params=params(),
    )(
        normed_grad,
        band,
        wb_t,
        pair_mid,
        pair_grad,
        pair_in,
        tri_sum,
        att_gain,
        tri_gain,
        sum_gain,
        w_tgate,
        w_tout,
        w_tout.T,
    )
    grad_planes = spread(sum_grad)

    def product(kernel, other):
        shape = (length, group, length) if split else (group, length, length)
        return pl.pallas_call(
            kernel,
            in_specs=[pl.BlockSpec(memory_space=pltpu.VMEM)] * 2,
            out_specs=pl.BlockSpec(memory_space=pltpu.VMEM),
            out_shape=jax.ShapeDtypeStruct(shape, BF16),
            compiler_params=pltpu.CompilerParams(vmem_limit_bytes=VMEM_BYTES),
        )(grad_planes, other)

    left_grad = collect(product(left_kernel, right_planes))
    right_grad = collect(product(right_kernel, left_planes))
    return run(
        functools.partial(final_kernel, split),
        (
            left_grad,
            right_grad,
            gate_back,
            mid_grad,
            pair_in,
            cell,
            tri_gain,
            wt_edges,
            w_left,
            w_right,
            w_tgate.T,
        ),
        6,
        row_shape,
        row_spec,
        special=((0, plane_spec), (1, plane_spec)),
    )


def solution(mesh):
    rows = P(("crop", "ia", "ja"), None, None)
    placed = (rows, rows, rows, rows, P("crop")) + (P(),) * 10
    return jax.shard_map(
        per_device, mesh=mesh, in_specs=placed, out_specs=rows, check_vma=False
    )
```
